32 devices in a mesh: sp: 32 (over z, y, x, core), ch: 1.
Axes of the slice: x: 2, y: 2, z: 4, core: 2. Of those that a mesh axis runs over, the one named last changes fastest.
Arguments:
- x_in: bfloat16 [256, 64, 128], P('ch', 'sp'), may hold values from -6 to 6
- gate_in: bfloat16 [256, 64, 128], P('ch', 'sp'), may hold values from -6 to 6
- conv_weight: float32 [256, 9], P('ch'), may hold values from -2 to 2
- conv_bias: float32 [256], P('ch'), may hold values from -0.5 to 0.5
- proj_weight: bfloat16 [4, 40, 256], P(None, None, 'ch'), may hold values from -0.375 to 0.375
- dt_weight: float32 [4, 256, 8], P(None, 'ch'), may hold values from -2 to 2
- dt_bias: float32 [4, 256], P(None, 'ch'), may hold values from -2 to 1
- decay_rate: float32 [4, 256, 16], P(None, 'ch'), may hold values from 0.0005 to 0.1
- skip_gain: float32 [4, 256], P(None, 'ch'), may hold values from 0.5 to 1.5
- norm_gain: float32 [256], P('ch'), may hold values from 0.5 to 1.5
- norm_bias: float32 [256], P('ch'), may hold values from -0.5 to 0.5
Outputs:
- mixed: bfloat16 [256, 64, 128], P('ch', 'sp')
The draws below stay inside these ranges and needn't reach their ends.
All inputs are finite; a program needn't handle non-finite values.
Results may differ from the reference program's by a relative error of at most 0.014.
Values may be sent and summed in bfloat16 or wider, within the bound.
A program may use at most 64 MiB of HBM per device.

```python
import math
import jax
import jax.numpy as jnp
from jax import lax

C = 256
N = 16
R = 8
H = 64
W = 128
N_CH = 1


def block_levels(key, shape, pieces, low, top_value):
    def one(axis_at, shards_of):
        steps = jax.random.uniform(jax.random.fold_in(jax.random.fold_in(key, 6), axis_at), (shards_of,), jnp.float32, low / len(pieces), top_value / len(pieces))
        return jnp.repeat(jnp.exp(steps), shape[axis_at] // shards_of).reshape((-1,) + (1,) * (len(shape) - axis_at - 1))

    level = one(*pieces[0])
    for cut in pieces[1:]:
        level = level * one(*cut)
    return level


def scatter_about(rng, shape, deviation, reach, pieces=(), dtype=jnp.bfloat16):
    entries = deviation * jax.random.normal(rng, shape, jnp.float32)
    if pieces:
        entries = entries * block_levels(rng, shape, pieces, -0.22, 0.18)
    return jnp.clip(entries, -reach, reach).astype(dtype)


def setup_inputs(seed: int = 0) -> dict:
    key_of = jax.random.split(jax.random.key(seed), 12)
    x_in = scatter_about(key_of[0], (C, H, W), 1.0, 6.0, ((1, 32),))
    gate_in = scatter_about(key_of[1], (C, H, W), 1.0, 6.0, ((1, 32),))
    conv_weight = scatter_about(key_of[2], (C, 9), 9 ** -0.5, 2.0, (), jnp.float32)
    conv_bias = jnp.clip(jax.random.uniform(key_of[3], (C,), jnp.float32, -0.5, 0.5), -0.5, 0.5)
    proj_weight = scatter_about(key_of[4], (4, R + 2 * N, C), C ** -0.5, 0.375)
    dt_weight = scatter_about(key_of[5], (4, C, R), R ** -0.5, 2.0, (), jnp.float32)
    dt_bias = jnp.clip(jax.random.uniform(key_of[6], (4, C), jnp.float32, -2.0, 1.0), -2.0, 1.0)
    decay_rate = jnp.clip(jnp.exp(jax.random.uniform(key_of[7], (4, C, N), jnp.float32, math.log(0.0005), math.log(0.1))), 0.0005, 0.1)
    skip_gain = jnp.clip(jax.random.uniform(key_of[8], (4, C), jnp.float32, 0.5, 1.5), 0.5, 1.5)
    norm_gain = jnp.clip(1.0 + 0.1 * jax.random.normal(key_of[9], (C,), jnp.float32), 0.5, 1.5)
    norm_bias = jnp.clip(jax.random.uniform(key_of[10], (C,), jnp.float32, -0.5, 0.5), -0.5, 0.5)
    return {"x_in": x_in, "gate_in": gate_in, "conv_weight": conv_weight, "conv_bias": conv_bias, "proj_weight": proj_weight, "dt_weight": dt_weight, "dt_bias": dt_bias, "decay_rate": decay_rate, "skip_gain": skip_gain, "norm_gain": norm_gain, "norm_bias": norm_bias}


def conv_silu(padded, conv_weight, conv_bias, rows, cols):
    total = jnp.zeros((padded.shape[0], rows, cols), jnp.float32) + conv_bias[:, None, None]
    for offset in range(9):
        down_shift = offset // 3
        side_shift = offset % 3
        window = padded[:, down_shift:down_shift + rows, side_shift:side_shift + cols].astype(jnp.float32)
        total = total + conv_weight[:, offset][:, None, None] * window
    return jax.nn.silu(total).astype(jnp.bfloat16)

def time_steps(low_rank, dt_weight, dt_bias):
    total = jnp.zeros(low_rank.shape[1:], jnp.float32)[None] + dt_bias[:, None, None]
    for rank_index in range(low_rank.shape[0]):
        total = total + dt_weight[:, rank_index][:, None, None] * low_rank[rank_index].astype(jnp.float32)[None]
    return jax.nn.softplus(total)

def line_scan(inputs, deltas, b_coef, c_coef, rates, skip_gain, reverse):
    moved = tuple((jnp.moveaxis(array, -1, 0) for array in (inputs, deltas, b_coef, c_coef)))

    def advance(states, items):
        values_now, delta_now, b_now, c_now = items
        decays = jnp.exp(-delta_now[:, None, :] * rates[:, :, None])
        states = decays * states + (delta_now * values_now)[:, None, :] * b_now[None, :, :]
        output = lax.optimization_barrier(jnp.sum(c_now[None, :, :] * states, axis=1)) + skip_gain[:, None] * values_now
        return (states, output)
    initial = jnp.zeros((inputs.shape[0], rates.shape[1], inputs.shape[1]), jnp.float32)
    _, outputs = lax.scan(advance, initial, moved, reverse=reverse)
    return jnp.moveaxis(outputs, 0, -1)

def projections(conv_out, proj_rows):
    chans, rows, cols = conv_out.shape
    group_size = chans // N_CH
    flattened = conv_out.reshape(chans, rows * cols)
    total = jnp.zeros((proj_rows.shape[0], rows * cols), jnp.float32)
    for group_index in range(N_CH):
        lower = group_index * group_size
        partial_sum = jnp.dot(proj_rows[:, lower:lower + group_size], flattened[lower:lower + group_size], preferred_element_type=jnp.float32)
        rounded = lax.optimization_barrier(partial_sum.astype(jnp.bfloat16))
        total = total + rounded.astype(jnp.float32)
    return total.astype(jnp.bfloat16).reshape(proj_rows.shape[0], rows, cols)

def reference(x_in, gate_in, conv_weight, conv_bias, proj_weight, dt_weight, dt_bias, decay_rate, skip_gain, norm_gain, norm_bias):
    chans, rows, cols = x_in.shape
    rank = dt_weight.shape[2]
    states = decay_rate.shape[2]
    width_proj = rank + 2 * states
    padded = jnp.pad(x_in, ((0, 0), (1, 1), (1, 1)))
    conv_out = conv_silu(padded, conv_weight, conv_bias, rows, cols)
    proj_all = projections(conv_out, proj_weight.reshape(4 * width_proj, chans)).reshape(4, width_proj, rows, cols)
    values = conv_out.astype(jnp.float32)
    horizontal = jnp.zeros((chans, rows, cols), jnp.float32)
    for direction in range(2):
        block = proj_all[direction]
        deltas = time_steps(block[:rank], dt_weight[direction], dt_bias[direction])
        horizontal = horizontal + line_scan(values, deltas, block[rank:rank + states].astype(jnp.float32), block[rank + states:].astype(jnp.float32), decay_rate[direction], skip_gain[direction], direction == 1)
    values_turned = values.transpose(0, 2, 1)
    vertical = jnp.zeros((chans, cols, rows), jnp.float32)
    for direction in range(2, 4):
        block = proj_all[direction].transpose(0, 2, 1)
        deltas = time_steps(block[:rank], dt_weight[direction], dt_bias[direction])
        vertical = vertical + line_scan(values_turned, deltas, block[rank:rank + states].astype(jnp.float32), block[rank + states:].astype(jnp.float32), decay_rate[direction], skip_gain[direction], direction == 3)
    vertical = lax.optimization_barrier(vertical.transpose(0, 2, 1).astype(jnp.bfloat16))
    combined = horizontal + vertical.astype(jnp.float32)
    mean = lax.optimization_barrier(jnp.sum(combined, axis=0)) / chans
    var = lax.optimization_barrier(jnp.sum(combined * combined, axis=0)) / chans - mean * mean
    normed = (combined - mean[None]) * lax.rsqrt(var[None] + 1e-05) * norm_gain[:, None, None] + norm_bias[:, None, None]
    return (normed * jax.nn.silu(gate_in.astype(jnp.float32))).astype(jnp.bfloat16)
```

```python
import functools

import jax
import jax.numpy as jnp
from jax import lax
from jax.experimental import pallas as pl
from jax.experimental.pallas import tpu as pltpu
from jax.sharding import PartitionSpec as P

SPAN = 64
MESH = pl.DeviceIdType.MESH
LOG2E = 1.4426950408889634
BEFORE = 64


def with_halo(value, sides, width):
    for axis, dim in sides:
        peers, length = (lax.axis_size(axis), value.shape[dim])
        up = [(i, (i + 1) % peers) for i in range(peers - 1)]
        down = [(j, i) for i, j in up]
        last = lax.slice_in_dim(value, length - width, length, axis=dim)
        first = lax.slice_in_dim(value, 0, width, axis=dim)
        before = lax.ppermute(last, axis, up)
        after = lax.ppermute(first, axis, down)
        value = jnp.concatenate([before, value, after], axis=dim)
    return value


def conv_silu(padded, conv_weight, conv_bias, rows, cols):
    total = jnp.zeros((padded.shape[0], rows, cols), jnp.float32) + conv_bias[:, None, None]
    for offset in range(9):
        down_shift = offset // 3
        side_shift = offset % 3
        window = padded[:, down_shift : down_shift + rows, side_shift : side_shift + cols].astype(
            jnp.float32
        )
        total = total + conv_weight[:, offset][:, None, None] * window
    return jax.nn.silu(total).astype(jnp.bfloat16)


def steps_first(low_rank, dt_weight, dt_bias):
    length, rank, lines = low_rank.shape
    total = jnp.zeros((length, dt_weight.shape[0], lines), jnp.float32) + dt_bias[None, :, None]
    for rank_index in range(rank):
        total = (
            total
            + dt_weight[:, rank_index][None, :, None]
            * low_rank[:, rank_index].astype(jnp.float32)[:, None, :]
        )
    return jax.nn.softplus(total)


def block_scan(values, low_rank, b_coef, c_coef, dt_weight, dt_bias, rates, skip_gain, reverse):
    length, chans, lines = values.shape
    states = rates.shape[1]
    block_len = min(SPAN, length)
    count = length // block_len
    deltas = steps_first(low_rank, dt_weight, dt_bias)
    rates_turned = rates.T[:, :, None]
    skip_column = skip_gain[:, None]

    def single(state, items):
        value_now, delta_now, b_now, c_now = items
        values_now = value_now.astype(jnp.float32)
        decays = jnp.exp(-delta_now[None] * rates_turned)
        state = (
            decays * state + (delta_now * values_now)[None] * b_now.astype(jnp.float32)[:, None, :]
        )
        output = (
            jnp.sum(c_now.astype(jnp.float32)[:, None, :] * state, axis=0)
            + skip_column * values_now
        )
        return (state, output)

    def advance(state, block_items):
        return lax.scan(single, state, block_items, reverse=reverse, unroll=block_len)

    items = (
        values.reshape(count, block_len, chans, lines),
        deltas.reshape(count, block_len, chans, lines),
        b_coef.reshape(count, block_len, states, lines),
        c_coef.reshape(count, block_len, states, lines),
    )
    initial = jnp.zeros((states, chans, lines), jnp.float32)
    _, outputs = lax.scan(advance, initial, items, reverse=reverse)
    return outputs.reshape(length, chans, lines)


def two_directions(values, proj_pair, dt_weight, dt_bias, decay_rate, skip_gain, first):
    rank = dt_weight.shape[2]
    states = decay_rate.shape[2]
    total = jnp.zeros(values.shape, jnp.float32)
    for offset in range(2):
        direction = first + offset
        block = proj_pair[offset]
        total = total + block_scan(
            values,
            block[:, :rank],
            block[:, rank : rank + states],
            block[:, rank + states :],
            dt_weight[direction],
            dt_bias[direction],
            decay_rate[direction],
            skip_gain[direction],
            offset == 1,
        )
    return total


def plain_device(
    x_in,
    gate_in,
    conv_weight,
    conv_bias,
    proj_weight,
    dt_weight,
    dt_bias,
    decay_rate,
    skip_gain,
    norm_gain,
    norm_bias,
):
    chans, rows, cols = x_in.shape
    rank = dt_weight.shape[2]
    states = decay_rate.shape[2]
    width_proj = rank + 2 * states
    padded = with_halo(x_in, (("sp", 1),), 1)
    padded = jnp.pad(padded, ((0, 0), (0, 0), (1, 1)))
    conv_out = conv_silu(padded, conv_weight, conv_bias, rows, cols)
    flattened = conv_out.reshape(chans, rows * cols)
    partial_sum = jnp.dot(
        proj_weight[:2].reshape(2 * width_proj, chans),
        flattened,
        preferred_element_type=jnp.float32,
    )
    row_proj = lax.psum(partial_sum.astype(jnp.bfloat16), "ch").reshape(2, width_proj, rows, cols)
    col_in = lax.all_to_all(conv_out, "sp", split_axis=2, concat_axis=1, tiled=True)
    col_flat = col_in.reshape(chans, col_in.shape[1] * col_in.shape[2])
    col_partial = jnp.dot(
        proj_weight[2:].reshape(2 * width_proj, chans), col_flat, preferred_element_type=jnp.float32
    )
    col_proj = lax.psum(col_partial.astype(jnp.bfloat16), "ch").reshape(
        2, width_proj, col_in.shape[1], col_in.shape[2]
    )
    row_values = conv_out.transpose(2, 0, 1)
    row_pair = row_proj.transpose(0, 3, 1, 2)
    horizontal = two_directions(
        row_values, row_pair, dt_weight, dt_bias, decay_rate, skip_gain, 0
    ).transpose(1, 2, 0)
    col_values = col_in.transpose(1, 0, 2)
    col_pair = col_proj.transpose(0, 2, 1, 3)
    vertical = two_directions(col_values, col_pair, dt_weight, dt_bias, decay_rate, skip_gain, 2)
    vertical = vertical.transpose(1, 0, 2).astype(jnp.bfloat16)
    vertical_rows = lax.all_to_all(vertical, "sp", split_axis=1, concat_axis=2, tiled=True)
    combined = horizontal + vertical_rows.astype(jnp.float32)
    sum_first, sum_second = lax.psum(
        (jnp.sum(combined, axis=0), jnp.sum(combined * combined, axis=0)), "ch"
    )
    chans_total = chans * lax.axis_size("ch")
    mean = sum_first / chans_total
    var = sum_second / chans_total - mean * mean
    normed = (combined - mean[None]) * lax.rsqrt(var[None] + 1e-05) * norm_gain[
        :, None, None
    ] + norm_bias[:, None, None]
    return (normed * jax.nn.silu(gate_in.astype(jnp.float32))).astype(jnp.bfloat16)


def fused_kernel(
    n,
    x_ref,
    cw_ref,
    cb_ref,
    pw_ref,
    dw_ref,
    db_ref,
    rate_ref,
    skip_ref,
    gain_ref,
    nbias_ref,
    out_ref,
    xpad,
    halo,
    xsend,
    xrecv,
    xv,
    cr,
    wf,
    wd,
    rate_h,
    rate_v,
    u_h,
    d_h,
    p_h,
    ya_h,
    yb_h,
    state_h,
    u_v,
    d_v,
    p_v,
    ya_v,
    yb_v,
    vsend,
    vrecv,
    halo_send,
    halo_recv,
    xs_sem,
    xr_sem,
    vs_sem,
    vr_sem,
):
    rows, cols, chans = x_ref.shape
    height = rows * n
    rank = dw_ref.shape[1]
    states = rate_ref.shape[1]
    width = rank + 2 * states
    half = states // 2
    f32, bf16 = jnp.float32, jnp.bfloat16
    me = lax.axis_index("sp")
    right, left = lax.rem(me + 1, n), lax.rem(me + n - 1, n)

    barrier = pltpu.get_barrier_semaphore()

    @pl.loop(1, n)
    def _(d):
        pl.semaphore_signal(
            barrier, inc=1, device_id={"sp": lax.rem(me + d, n)}, device_id_type=MESH
        )

    edge = jnp.zeros((rows + 2, 8, chans), f32)
    xpad[:, 0:8, :] = edge
    xpad[:, cols + 8 : cols + 16, :] = edge
    for r in range(rows):
        xpad[r + 1, 8 : cols + 8, :] = x_ref[r].astype(f32)
    for j in range(n):
        at = 8 + 4 * j - 2
        pair = [xpad[r + 1, at : at + 8, :] for r in range(rows)]
        xsend[j] = jnp.concatenate(pair, axis=0).astype(bf16)
    xrecv[pl.ds(me, 1)] = xsend[pl.ds(me, 1)]

    pl.semaphore_wait(barrier, n - 1)

    def halo_copy(which):
        return pltpu.make_async_remote_copy(
            src_ref=x_ref.at[rows - 1 if which == 0 else 0],
            dst_ref=halo.at[which],
            send_sem=halo_send.at[which],
            recv_sem=halo_recv.at[which],
            device_id={"sp": right if which == 0 else left},
            device_id_type=MESH,
        )

    halo_copy(0).start()
    halo_copy(1).start()

    def x_copy(d, slot):
        dst = lax.rem(me + d, n)
        return pltpu.make_async_remote_copy(
            src_ref=xsend.at[dst],
            dst_ref=xrecv.at[slot],
            send_sem=xs_sem.at[d],
            recv_sem=xr_sem.at[d],
            device_id={"sp": dst},
            device_id_type=MESH,
        )

    def v_copy(d, slot):
        dst = lax.rem(me + d, n)
        return pltpu.make_async_remote_copy(
            src_ref=vsend.at[dst],
            dst_ref=vrecv.at[slot],
            send_sem=vs_sem.at[d],
            recv_sem=vr_sem.at[d],
            device_id={"sp": dst},
            device_id_type=MESH,
        )

    @pl.loop(1, n)
    def _(d):
        x_copy(d, me).start()

    sub = lax.broadcasted_iota(jnp.int32, (8, chans), 0)
    low4 = sub < 4
    dir_h = (sub // 2) % 2 == 0
    dir_v = low4
    low4_one = lax.broadcasted_iota(jnp.int32, (8, 128), 0) < 4

    wf[...] = jnp.zeros(wf.shape, f32)
    wd[...] = jnp.zeros(wd.shape, f32)
    for k in range(4):
        base = 128 * k
        rowsw = pw_ref[k].astype(f32)
        wf[base : base + width, :] = rowsw
        wf[base + width : base + width + rank, :] = rowsw[0:rank]
        full = dw_ref[k]
        high = full.astype(bf16).astype(f32)
        wd[base : base + rank, :] = high
        wd[base + width : base + width + rank, :] = full - high
    for s in range(states):
        rate_v[s] = -LOG2E * jnp.where(
            dir_v, rate_ref[2, s : s + 1, :], rate_ref[3, s : s + 1, :]
        )
    for s in range(half):
        lower = jnp.where(dir_h, rate_ref[0, s : s + 1, :], rate_ref[1, s : s + 1, :])
        upper = jnp.where(
            dir_h, rate_ref[0, s + half : s + half + 1, :], rate_ref[1, s + half : s + half + 1, :]
        )
        rate_h[s] = -LOG2E * jnp.where(low4, lower, upper)

    def prepare(steps, first, dirs, u, dl, p, halves):
        weights = wf[256 * first : 256 * first + 256, :].astype(bf16)
        up = wd[256 * first : 256 * first + 256, :].astype(bf16)
        bias = jnp.where(dirs, db_ref[2 * first : 2 * first + 1], db_ref[2 * first + 1 : 2 * first + 2])
        bias = bias[None]
        pick = dirs[:, 0:128][None]
        lift = low4_one[None]
        size = 16

        @pl.loop(0, steps // size)
        def _(i):
            at = pl.ds(i * size, size)
            flat = u[at].reshape(size * 8, chans).astype(bf16)
            proj = lax.dot_general(
                flat, weights, (((1,), (1,)), ((), ())), preferred_element_type=f32
            )
            proj = proj.astype(bf16).astype(f32).reshape(size, 8, 256)
            one, two = proj[:, :, 0:128], proj[:, :, 128:256]
            own = jnp.where(pick, one, two)
            both = jnp.concatenate(
                [jnp.where(pick, one, 0.0), jnp.where(pick, 0.0, two)], axis=2
            )
            pre = jnp.dot(
                both.reshape(size * 8, 256).astype(bf16), up, preferred_element_type=f32
            ).reshape(size, 8, chans)
            pre = pre + bias
            dl[at] = jnp.maximum(pre, 0.0) + jnp.log1p(jnp.exp(-jnp.abs(pre)))
            if halves:
                own = jnp.where(lift, own, pltpu.roll(own, 128 - half, 2))
            p[at] = own

    def step(t, state, u, dl, p, rate, ya, yb, last, count, offset):
        delta, tile = dl[t], p[t]
        drive = delta * u[t]
        total = None
        new = []
        for s in range(count):
            decay = jnp.exp2(delta * rate[s])
            b_now = jnp.broadcast_to(tile[:, rank + s : rank + s + 1], (8, chans))
            c_now = jnp.broadcast_to(tile[:, offset + s : offset + s + 1], (8, chans))
            now = decay * state[s] + drive * b_now
            new.append(now)
            term = c_now * now
            total = term if total is None else total + term
        for k in range(chans // 128):
            piece = total[:, k * 128 : k * 128 + 128]
            ya[k, pl.ds(pl.multiple_of(t * 8, 8), 8), :] = piece
            yb[k, pl.ds(pl.multiple_of((last - t) * 8, 8), 8), :] = piece
        return tuple(new)

    for which in range(2):
        halo_copy(which).wait()
    above, below = halo[0].astype(f32), halo[1].astype(f32)
    xpad[0, 8 : cols + 8, :] = jnp.where(me == 0, jnp.zeros_like(above), above)
    xpad[rows + 1, 8 : cols + 8, :] = jnp.where(me == n - 1, jnp.zeros_like(below), below)
    block = 32
    for r in range(rows):
        for c in range(0, cols, block):
            total = jnp.zeros((block, chans), f32) + cb_ref[...]
            for i in range(3):
                for j in range(3):
                    window = xpad[r + i, 7 + c + j : 7 + c + j + block, :]
                    total = total + cw_ref[3 * i + j : 3 * i + j + 1, :] * window
            cr[r, c : c + block, :] = jax.nn.silu(total).astype(bf16).astype(f32)

    odd = sub % 2 == 1

    def spread(t):
        ahead = jnp.where(odd, cr[1, pl.ds(t, 1), :], cr[0, pl.ds(t, 1), :])
        back = jnp.where(odd, cr[1, pl.ds(cols - 1 - t, 1), :], cr[0, pl.ds(cols - 1 - t, 1), :])
        u_h[t] = jnp.where(dir_h, ahead, back)

    @pl.loop(0, cols // 8)
    def _(i):
        for k in range(8):
            spread(i * 8 + k)

    prepare(cols, 0, dir_h, u_h, d_h, p_h, True)

    def row_steps(lower, upper, state):
        def body(t, state):
            return step(
                t, state, u_h, d_h, p_h, rate_h, ya_h, yb_h, cols - 1, half, rank + states
            )

        return lax.fori_loop(lower, upper, body, state, unroll=2)

    state = row_steps(0, BEFORE, tuple(jnp.zeros((8, chans), f32) for _ in range(half)))
    for s in range(half):
        state_h[s] = state[s]

    @pl.loop(1, n)
    def _(d):
        x_copy(d, lax.rem(me + n - d, n)).wait()

    nothing = jnp.zeros((8, chans), f32)
    xv[0] = nothing
    xv[height + 1] = nothing

    @pl.loop(0, n)
    def _(j):
        both = xrecv[j].astype(f32)
        xv[1 + 2 * j] = both[0:8]
        xv[2 + 2 * j] = both[8:16]

    def conv_step(t):
        total = jnp.zeros((8, chans), f32) + cb_ref[...]
        tiles = [xv[t], xv[t + 1], xv[t + 2]]
        for j in range(3):
            part = None
            for i in range(3):
                term = cw_ref[3 * i + j : 3 * i + j + 1, :] * tiles[i]
                part = term if part is None else part + term
            total = total + pltpu.roll(part, 7 - j, 0)
        value = jax.nn.silu(total).astype(bf16).astype(f32)
        turned = pltpu.roll(value, 4, 0)
        u_v[t, 0:4, :] = value[0:4]
        u_v[height - 1 - t, 4:8, :] = turned[4:8]

    @pl.loop(0, height // 4)
    def _(i):
        for k in range(4):
            conv_step(i * 4 + k)

    prepare(height, 1, dir_v, u_v, d_v, p_v, False)

    def col_body(t, state):
        return step(
            t, state, u_v, d_v, p_v, rate_v, ya_v, yb_v, height - 1, states, rank + states
        )

    lax.fori_loop(
        0, height, col_body, tuple(jnp.zeros((8, chans), f32) for _ in range(states)), unroll=2
    )

    skip_v = skip_ref[2:3, :] + skip_ref[3:4, :]

    def column_row(t):
        at = pl.ds(pl.multiple_of(t * 8, 8), 8)
        parts = [
            ya_v[k, at, :] + pltpu.roll(yb_v[k, at, :], 4, 0) for k in range(chans // 128)
        ]
        return jnp.concatenate(parts, axis=1) + skip_v * u_v[t]

    def column_tile(j):
        tile = jnp.where(low4, column_row(2 * j), pltpu.roll(column_row(2 * j + 1), 4, 0))
        return jnp.concatenate([tile[:, 0:128], tile[:, 128:256]], axis=0).astype(bf16)

    @pl.loop(1, n)
    def _(d):
        j = lax.rem(me + d, n)
        vsend[j] = column_tile(j)
        v_copy(d, me).start()

    vrecv[me] = column_tile(me)

    row_steps(BEFORE, cols, tuple(state_h[s] for s in range(half)))

    @pl.loop(1, n)
    def _(d):
        v_copy(d, lax.rem(me + n - d, n)).wait()

    skip_h = skip_ref[0:1, :] + skip_ref[1:2, :]

    def finish(p):
        even, other = vrecv[2 * p].astype(f32), vrecv[2 * p + 1].astype(f32)
        even = jnp.concatenate([even[0:8], even[8:16]], axis=1)
        other = jnp.concatenate([other[0:8], other[8:16]], axis=1)
        at = pl.ds(pl.multiple_of(p * 8, 8), 8)
        for r in range(rows):
            if r == 0:
                upright = jnp.where(low4, even, pltpu.roll(other, 4, 0))
            else:
                upright = jnp.where(low4, pltpu.roll(even, 4, 0), other)
            flat = skip_h * cr[r, at, :]
            for source, line in ((ya_h, r), (ya_h, 4 + r), (yb_h, 2 + r), (yb_h, 6 + r)):
                parts = [
                    source[k, pl.ds(p * 64 + line, 8, stride=8), :]
                    for k in range(chans // 128)
                ]
                flat = flat + jnp.concatenate(parts, axis=1)
            combined = flat + upright
            mean = jnp.sum(combined, axis=1, keepdims=True) / chans
            var = jnp.sum(combined * combined, axis=1, keepdims=True) / chans - mean * mean
            normed = (combined - mean) * lax.rsqrt(var + 1e-05)
            out_ref[r, at, :] = normed * gain_ref[...] + nbias_ref[...]

    @pl.loop(0, cols // 16)
    def _(i):
        finish(2 * i)
        finish(2 * i + 1)


def fused_device(
    n,
    x_in,
    gate_in,
    conv_weight,
    conv_bias,
    proj_weight,
    dt_weight,
    dt_bias,
    decay_rate,
    skip_gain,
    norm_gain,
    norm_bias,
):
    chans, rows, cols = x_in.shape
    states = decay_rate.shape[2]
    height = rows * n
    f32, bf16 = jnp.float32, jnp.bfloat16
    scratch = [
        pltpu.VMEM((rows + 2, cols + 16, chans), f32),
        pltpu.VMEM((2, cols, chans), bf16),
        pltpu.VMEM((n, 16, chans), bf16),
        pltpu.VMEM((n, 16, chans), bf16),
        pltpu.VMEM((height + 2, 8, chans), f32),
        pltpu.VMEM((rows, cols, chans), f32),
        pltpu.VMEM((512, chans), f32),
        pltpu.VMEM((512, chans), f32),
        pltpu.VMEM((states // 2, 8, chans), f32),
        pltpu.VMEM((states, 8, chans), f32),
        pltpu.VMEM((cols, 8, chans), f32),
        pltpu.VMEM((cols, 8, chans), f32),
        pltpu.VMEM((cols, 8, 128), f32),
        pltpu.VMEM((chans // 128, cols * 8, 128), f32),
        pltpu.VMEM((chans // 128, cols * 8, 128), f32),
        pltpu.VMEM((states // 2, 8, chans), f32),
        pltpu.VMEM((height, 8, chans), f32),
        pltpu.VMEM((height, 8, chans), f32),
        pltpu.VMEM((height, 8, 128), f32),
        pltpu.VMEM((chans // 128, height * 8, 128), f32),
        pltpu.VMEM((chans // 128, height * 8, 128), f32),
        pltpu.VMEM((n, 16, 128), bf16),
        pltpu.VMEM((n, 16, 128), bf16),
        pltpu.SemaphoreType.DMA((2,)),
        pltpu.SemaphoreType.DMA((2,)),
        pltpu.SemaphoreType.DMA((n,)),
        pltpu.SemaphoreType.DMA((n,)),
        pltpu.SemaphoreType.DMA((n,)),
        pltpu.SemaphoreType.DMA((n,)),
    ]
    normed = pl.pallas_call(
        functools.partial(fused_kernel, n),
        out_shape=jax.ShapeDtypeStruct((rows, cols, chans), f32),
        in_specs=[pl.BlockSpec(memory_space=pltpu.VMEM)] * 10,
        out_specs=pl.BlockSpec(memory_space=pltpu.VMEM),
        scratch_shapes=scratch,
        compiler_params=pltpu.CompilerParams(
            collective_id=0, has_side_effects=True, vmem_limit_bytes=40 * 1024 * 1024
        ),
    )(
        x_in.transpose(1, 2, 0),
        conv_weight.T,
        conv_bias[None, :],
        proj_weight,
        dt_weight.transpose(0, 2, 1),
        dt_bias,
        decay_rate.transpose(0, 2, 1),
        skip_gain,
        norm_gain[None, :],
        norm_bias[None, :],
    )
    gate = jax.nn.silu(gate_in.astype(f32))
    return (normed.transpose(2, 0, 1) * gate).astype(bf16)


def on_device(*args):
    n = lax.axis_size("sp")
    chans, rows, cols = args[0].shape
    rank, states = args[5].shape[2], args[7].shape[2]
    fits = (chans, rows, cols, rank, states) == (256, 2, 4 * n, 8, 16)
    if lax.axis_size("ch") == 1 and fits:
        return fused_device(n, *args)
    return plain_device(*args)


def solution(mesh):
    placed = (
        P("ch", "sp", None),
        P("ch", "sp", None),
        P("ch", None),
        P("ch"),
        P(None, None, "ch"),
        P(None, "ch", None),
        P(None, "ch"),
        P(None, "ch", None),
        P(None, "ch"),
        P("ch"),
        P("ch"),
    )
    return jax.shard_map(
        on_device, mesh=mesh, in_specs=placed, out_specs=P("ch", "sp", None), check_vma=False
    )
```

```python
import functools

import jax
import jax.numpy as jnp
from jax import lax
from jax.experimental import pallas as pl
from jax.experimental.pallas import tpu as pltpu
from jax.sharding import PartitionSpec as P

SPAN = 64
MESH = pl.DeviceIdType.MESH
UNROLL = 8
BEFORE = 64


def with_halo(value, sides, width):
    for axis, dim in sides:
        peers, length = (lax.axis_size(axis), value.shape[dim])
        up = [(i, (i + 1) % peers) for i in range(peers - 1)]
        down = [(j, i) for i, j in up]
        last = lax.slice_in_dim(value, length - width, length, axis=dim)
        first = lax.slice_in_dim(value, 0, width, axis=dim)
        before = lax.ppermute(last, axis, up)
        after = lax.ppermute(first, axis, down)
        value = jnp.concatenate([before, value, after], axis=dim)
    return value


def conv_silu(padded, conv_weight, conv_bias, rows, cols):
    total = jnp.zeros((padded.shape[0], rows, cols), jnp.float32) + conv_bias[:, None, None]
    for offset in range(9):
        down_shift = offset // 3
        side_shift = offset % 3
        window = padded[:, down_shift : down_shift + rows, side_shift : side_shift + cols].astype(
            jnp.float32
        )
        total = total + conv_weight[:, offset][:, None, None] * window
    return jax.nn.silu(total).astype(jnp.bfloat16)


def steps_first(low_rank, dt_weight, dt_bias):
    length, rank, lines = low_rank.shape
    total = jnp.zeros((length, dt_weight.shape[0], lines), jnp.float32) + dt_bias[None, :, None]
    for rank_index in range(rank):
        total = (
            total
            + dt_weight[:, rank_index][None, :, None]
            * low_rank[:, rank_index].astype(jnp.float32)[:, None, :]
        )
    return jax.nn.softplus(total)


def block_scan(values, low_rank, b_coef, c_coef, dt_weight, dt_bias, rates, skip_gain, reverse):
    length, chans, lines = values.shape
    states = rates.shape[1]
    block_len = min(SPAN, length)
    count = length // block_len
    deltas = steps_first(low_rank, dt_weight, dt_bias)
    rates_turned = rates.T[:, :, None]
    skip_column = skip_gain[:, None]

    def single(state, items):
        value_now, delta_now, b_now, c_now = items
        values_now = value_now.astype(jnp.float32)
        decays = jnp.exp(-delta_now[None] * rates_turned)
        state = (
            decays * state + (delta_now * values_now)[None] * b_now.astype(jnp.float32)[:, None, :]
        )
        output = (
            jnp.sum(c_now.astype(jnp.float32)[:, None, :] * state, axis=0)
            + skip_column * values_now
        )
        return (state, output)

    def advance(state, block_items):
        return lax.scan(single, state, block_items, reverse=reverse, unroll=block_len)

    items = (
        values.reshape(count, block_len, chans, lines),
        deltas.reshape(count, block_len, chans, lines),
        b_coef.reshape(count, block_len, states, lines),
        c_coef.reshape(count, block_len, states, lines),
    )
    initial = jnp.zeros((states, chans, lines), jnp.float32)
    _, outputs = lax.scan(advance, initial, items, reverse=reverse)
    return outputs.reshape(length, chans, lines)


def two_directions(values, proj_pair, dt_weight, dt_bias, decay_rate, skip_gain, first):
    rank = dt_weight.shape[2]
    states = decay_rate.shape[2]
    total = jnp.zeros(values.shape, jnp.float32)
    for offset in range(2):
        direction = first + offset
        block = proj_pair[offset]
        total = total + block_scan(
            values,
            block[:, :rank],
            block[:, rank : rank + states],
            block[:, rank + states :],
            dt_weight[direction],
            dt_bias[direction],
            decay_rate[direction],
            skip_gain[direction],
            offset == 1,
        )
    return total


def plain_device(
    x_in,
    gate_in,
    conv_weight,
    conv_bias,
    proj_weight,
    dt_weight,
    dt_bias,
    decay_rate,
    skip_gain,
    norm_gain,
    norm_bias,
):
    chans, rows, cols = x_in.shape
    rank = dt_weight.shape[2]
    states = decay_rate.shape[2]
    width_proj = rank + 2 * states
    padded = with_halo(x_in, (("sp", 1),), 1)
    padded = jnp.pad(padded, ((0, 0), (0, 0), (1, 1)))
    conv_out = conv_silu(padded, conv_weight, conv_bias, rows, cols)
    flattened = conv_out.reshape(chans, rows * cols)
    partial_sum = jnp.dot(
        proj_weight[:2].reshape(2 * width_proj, chans),
        flattened,
        preferred_element_type=jnp.float32,
    )
    row_proj = lax.psum(partial_sum.astype(jnp.bfloat16), "ch").reshape(2, width_proj, rows, cols)
    col_in = lax.all_to_all(conv_out, "sp", split_axis=2, concat_axis=1, tiled=True)
    col_flat = col_in.reshape(chans, col_in.shape[1] * col_in.shape[2])
    col_partial = jnp.dot(
        proj_weight[2:].reshape(2 * width_proj, chans), col_flat, preferred_element_type=jnp.float32
    )
    col_proj = lax.psum(col_partial.astype(jnp.bfloat16), "ch").reshape(
        2, width_proj, col_in.shape[1], col_in.shape[2]
    )
    row_values = conv_out.transpose(2, 0, 1)
    row_pair = row_proj.transpose(0, 3, 1, 2)
    horizontal = two_directions(
        row_values, row_pair, dt_weight, dt_bias, decay_rate, skip_gain, 0
    ).transpose(1, 2, 0)
    col_values = col_in.transpose(1, 0, 2)
    col_pair = col_proj.transpose(0, 2, 1, 3)
    vertical = two_directions(col_values, col_pair, dt_weight, dt_bias, decay_rate, skip_gain, 2)
    vertical = vertical.transpose(1, 0, 2).astype(jnp.bfloat16)
    vertical_rows = lax.all_to_all(vertical, "sp", split_axis=1, concat_axis=2, tiled=True)
    combined = horizontal + vertical_rows.astype(jnp.float32)
    sum_first, sum_second = lax.psum(
        (jnp.sum(combined, axis=0), jnp.sum(combined * combined, axis=0)), "ch"
    )
    chans_total = chans * lax.axis_size("ch")
    mean = sum_first / chans_total
    var = sum_second / chans_total - mean * mean
    normed = (combined - mean[None]) * lax.rsqrt(var[None] + 1e-05) * norm_gain[
        :, None, None
    ] + norm_bias[:, None, None]
    return (normed * jax.nn.silu(gate_in.astype(jnp.float32))).astype(jnp.bfloat16)


def fused_kernel(
    n,
    x_ref,
    cw_ref,
    cb_ref,
    pw_ref,
    dw_ref,
    db_ref,
    rate_ref,
    skip_ref,
    gain_ref,
    nbias_ref,
    out_ref,
    xpad,
    halo,
    xsend,
    xrecv,
    xv,
    cr,
    wf,
    wt,
    wd,
    rate_h,
    rate_v,
    u_h,
    d_h,
    p_h,
    ya_h,
    yb_h,
    state_h,
    u_v,
    d_v,
    p_v,
    ya_v,
    yb_v,
    vsend,
    vrecv,
    halo_send,
    halo_recv,
    xs_sem,
    xr_sem,
    vs_sem,
    vr_sem,
):
    rows, cols, chans = x_ref.shape
    height = rows * n
    rank = dw_ref.shape[1]
    states = rate_ref.shape[1]
    width = rank + 2 * states
    half = states // 2
    f32, bf16 = jnp.float32, jnp.bfloat16
    me = lax.axis_index("sp")
    right, left = lax.rem(me + 1, n), lax.rem(me + n - 1, n)

    barrier = pltpu.get_barrier_semaphore()

    @pl.loop(1, n)
    def _(d):
        pl.semaphore_signal(
            barrier, inc=1, device_id={"sp": lax.rem(me + d, n)}, device_id_type=MESH
        )

    edge = jnp.zeros((rows + 2, 8, chans), f32)
    xpad[:, 0:8, :] = edge
    xpad[:, cols + 8 : cols + 16, :] = edge
    for r in range(rows):
        xpad[r + 1, 8 : cols + 8, :] = x_ref[r].astype(f32)
    for j in range(n):
        at = 8 + 4 * j - 2
        pair = [xpad[r + 1, at : at + 8, :] for r in range(rows)]
        xsend[j] = jnp.concatenate(pair, axis=0).astype(bf16)
    xrecv[pl.ds(me, 1)] = xsend[pl.ds(me, 1)]

    pl.semaphore_wait(barrier, n - 1)

    def halo_copy(which):
        return pltpu.make_async_remote_copy(
            src_ref=x_ref.at[rows - 1 if which == 0 else 0],
            dst_ref=halo.at[which],
            send_sem=halo_send.at[which],
            recv_sem=halo_recv.at[which],
            device_id={"sp": right if which == 0 else left},
            device_id_type=MESH,
        )

    halo_copy(0).start()
    halo_copy(1).start()

    def x_copy(d, slot):
        dst = lax.rem(me + d, n)
        return pltpu.make_async_remote_copy(
            src_ref=xsend.at[dst],
            dst_ref=xrecv.at[slot],
            send_sem=xs_sem.at[d],
            recv_sem=xr_sem.at[d],
            device_id={"sp": dst},
            device_id_type=MESH,
        )

    def v_copy(d, slot):
        dst = lax.rem(me + d, n)
        return pltpu.make_async_remote_copy(
            src_ref=vsend.at[dst],
            dst_ref=vrecv.at[slot],
            send_sem=vs_sem.at[d],
            recv_sem=vr_sem.at[d],
            device_id={"sp": dst},
            device_id_type=MESH,
        )

    @pl.loop(1, n)
    def _(d):
        x_copy(d, me).start()

    sub = lax.broadcasted_iota(jnp.int32, (8, chans), 0)
    low4 = sub < 4
    dir_h = (sub // 2) % 2 == 0
    dir_v = low4
    low4_one = lax.broadcasted_iota(jnp.int32, (8, 128), 0) < 4

    wf[...] = jnp.zeros(wf.shape, f32)
    wd[...] = jnp.zeros(wd.shape, f32)
    for k in range(4):
        base = 128 * k
        rowsw = pw_ref[k].astype(f32)
        wf[base : base + width, :] = rowsw
        wf[base + width : base + width + rank, :] = rowsw[0:rank]
        full = dw_ref[k]
        high = full.astype(bf16).astype(f32)
        wd[base : base + rank, :] = high
        wd[base + width : base + width + rank, :] = full - high
    for first in range(2):
        wt[first] = wf[256 * first : 256 * first + 256, :].T.astype(bf16)
    for s in range(states):
        rate_v[s] = -jnp.where(
            dir_v, rate_ref[2, s : s + 1, :], rate_ref[3, s : s + 1, :]
        )
    for s in range(half):
        lower = jnp.where(dir_h, rate_ref[0, s : s + 1, :], rate_ref[1, s : s + 1, :])
        upper = jnp.where(
            dir_h, rate_ref[0, s + half : s + half + 1, :], rate_ref[1, s + half : s + half + 1, :]
        )
        rate_h[s] = -jnp.where(low4, lower, upper)

    def prepare(steps, first, dirs, u, dl, p, halves):
        weights = wt[first]
        up = wd[256 * first : 256 * first + 256, :].astype(bf16)
        bias = jnp.where(dirs, db_ref[2 * first : 2 * first + 1], db_ref[2 * first + 1 : 2 * first + 2])
        bias = bias[None]
        pick = dirs[:, 0:128][None]
        lift = low4_one[None]
        size = 32

        @pl.loop(0, steps // size)
        def _(i):
            at = pl.ds(i * size, size)
            flat = u[at].reshape(size * 8, chans).astype(bf16)
            proj = lax.dot_general(
                flat, weights, (((1,), (0,)), ((), ())), preferred_element_type=f32
            )
            proj = proj.astype(bf16).astype(f32).reshape(size, 8, 256)
            one, two = proj[:, :, 0:128], proj[:, :, 128:256]
            own = jnp.where(pick, one, two)
            both = jnp.concatenate(
                [jnp.where(pick, one, 0.0), jnp.where(pick, 0.0, two)], axis=2
            )
            pre = jnp.dot(
                both.reshape(size * 8, 256).astype(bf16), up, preferred_element_type=f32
            ).reshape(size, 8, chans)
            pre = pre + bias
            dl[at] = jnp.maximum(pre, 0.0) + jnp.log(1.0 + jnp.exp(-jnp.abs(pre)))
            if halves:
                own = jnp.where(lift, own, pltpu.roll(own, 128 - half, 2))
            p[at] = own

    def step(t, state, u, dl, p, rate, ya, yb, last, count, offset):
        delta, tile = dl[t], p[t]
        drive = delta * u[t]
        total = None
        new = []
        for s in range(count):
            decay = jnp.exp(delta * rate[s])
            b_now = jnp.broadcast_to(tile[:, rank + s : rank + s + 1], (8, chans))
            c_now = jnp.broadcast_to(tile[:, offset + s : offset + s + 1], (8, chans))
            now = decay * state[s] + drive * b_now
            new.append(now)
            term = c_now * now
            total = term if total is None else total + term
        for k in range(chans // 128):
            piece = total[:, k * 128 : k * 128 + 128]
            ya[k, pl.ds(pl.multiple_of(t * 8, 8), 8), :] = piece
            yb[k, pl.ds(pl.multiple_of((last - t) * 8, 8), 8), :] = piece
        return tuple(new)

    for which in range(2):
        halo_copy(which).wait()
    above, below = halo[0].astype(f32), halo[1].astype(f32)
    xpad[0, 8 : cols + 8, :] = jnp.where(me == 0, jnp.zeros_like(above), above)
    xpad[rows + 1, 8 : cols + 8, :] = jnp.where(me == n - 1, jnp.zeros_like(below), below)
    block = 32
    for r in range(rows):
        for c in range(0, cols, block):
            total = jnp.zeros((block, chans), f32) + cb_ref[...]
            for i in range(3):
                for j in range(3):
                    window = xpad[r + i, 7 + c + j : 7 + c + j + block, :]
                    total = total + cw_ref[3 * i + j : 3 * i + j + 1, :] * window
            cr[r, c : c + block, :] = jax.nn.silu(total).astype(bf16).astype(f32)

    odd = sub % 2 == 1

    def spread(t):
        ahead = jnp.where(odd, cr[1, pl.ds(t, 1), :], cr[0, pl.ds(t, 1), :])
        back = jnp.where(odd, cr[1, pl.ds(cols - 1 - t, 1), :], cr[0, pl.ds(cols - 1 - t, 1), :])
        u_h[t] = jnp.where(dir_h, ahead, back)

    @pl.loop(0, cols // 8)
    def _(i):
        for k in range(8):
            spread(i * 8 + k)

    prepare(cols, 0, dir_h, u_h, d_h, p_h, True)

    def row_steps(lower, upper, state):
        def body(t, state):
            return step(
                t, state, u_h, d_h, p_h, rate_h, ya_h, yb_h, cols - 1, half, rank + states
            )

        return lax.fori_loop(lower, upper, body, state, unroll=UNROLL)

    state = row_steps(0, BEFORE, tuple(jnp.zeros((8, chans), f32) for _ in range(half)))
    for s in range(half):
        state_h[s] = state[s]

    @pl.loop(1, n)
    def _(d):
        x_copy(d, lax.rem(me + n - d, n)).wait()

    nothing = jnp.zeros((8, chans), f32)
    xv[0] = nothing
    xv[height + 1] = nothing

    @pl.loop(0, n)
    def _(j):
        both = xrecv[j].astype(f32)
        xv[1 + 2 * j] = both[0:8]
        xv[2 + 2 * j] = both[8:16]

    def conv_step(t):
        total = jnp.zeros((8, chans), f32) + cb_ref[...]
        tiles = [xv[t], xv[t + 1], xv[t + 2]]
        for j in range(3):
            part = None
            for i in range(3):
                term = cw_ref[3 * i + j : 3 * i + j + 1, :] * tiles[i]
                part = term if part is None else part + term
            total = total + pltpu.roll(part, 7 - j, 0)
        value = jax.nn.silu(total).astype(bf16).astype(f32)
        turned = pltpu.roll(value, 4, 0)
        u_v[t, 0:4, :] = value[0:4]
        u_v[height - 1 - t, 4:8, :] = turned[4:8]

    @pl.loop(0, height // 8)
    def _(i):
        for k in range(8):
            conv_step(i * 8 + k)

    prepare(height, 1, dir_v, u_v, d_v, p_v, False)

    def col_body(t, state):
        return step(
            t, state, u_v, d_v, p_v, rate_v, ya_v, yb_v, height - 1, states, rank + states
        )

    lax.fori_loop(
        0, height, col_body, tuple(jnp.zeros((8, chans), f32) for _ in range(states)), unroll=UNROLL
    )

    skip_v = skip_ref[2:3, :] + skip_ref[3:4, :]

    def column_row(t):
        at = pl.ds(pl.multiple_of(t * 8, 8), 8)
        parts = [
            ya_v[k, at, :] + pltpu.roll(yb_v[k, at, :], 4, 0) for k in range(chans // 128)
        ]
        return jnp.concatenate(parts, axis=1) + skip_v * u_v[t]

    def column_tile(j):
        tile = jnp.where(low4, column_row(2 * j), pltpu.roll(column_row(2 * j + 1), 4, 0))
        return jnp.concatenate([tile[:, 0:128], tile[:, 128:256]], axis=0).astype(bf16)

    @pl.loop(0, n // 8)
    def _(i):
        for k in range(8):
            vsend[i * 8 + k] = column_tile(i * 8 + k)

    @pl.loop(1, n)
    def _(d):
        v_copy(d, me).start()

    vrecv[pl.ds(me, 1)] = vsend[pl.ds(me, 1)]

    row_steps(BEFORE, cols, tuple(state_h[s] for s in range(half)))

    @pl.loop(1, n)
    def _(d):
        v_copy(d, lax.rem(me + n - d, n)).wait()

    skip_h = skip_ref[0:1, :] + skip_ref[1:2, :]

    def finish(p):
        even, other = vrecv[2 * p].astype(f32), vrecv[2 * p + 1].astype(f32)
        even = jnp.concatenate([even[0:8], even[8:16]], axis=1)
        other = jnp.concatenate([other[0:8], other[8:16]], axis=1)
        at = pl.ds(pl.multiple_of(p * 8, 8), 8)
        for r in range(rows):
            if r == 0:
                upright = jnp.where(low4, even, pltpu.roll(other, 4, 0))
            else:
                upright = jnp.where(low4, pltpu.roll(even, 4, 0), other)
            flat = skip_h * cr[r, at, :]
            for source, line in ((ya_h, r), (ya_h, 4 + r), (yb_h, 2 + r), (yb_h, 6 + r)):
                parts = [
                    source[k, pl.ds(p * 64 + line, 8, stride=8), :]
                    for k in range(chans // 128)
                ]
                flat = flat + jnp.concatenate(parts, axis=1)
            combined = flat + upright
            mean = jnp.sum(combined, axis=1, keepdims=True) / chans
            var = jnp.sum(combined * combined, axis=1, keepdims=True) / chans - mean * mean
            normed = (combined - mean) * lax.rsqrt(var + 1e-05)
            out_ref[r, at, :] = normed * gain_ref[...] + nbias_ref[...]

    @pl.loop(0, cols // 32)
    def _(i):
        for k in range(4):
            finish(4 * i + k)


def fused_device(
    n,
    x_in,
    gate_in,
    conv_weight,
    conv_bias,
    proj_weight,
    dt_weight,
    dt_bias,
    decay_rate,
    skip_gain,
    norm_gain,
    norm_bias,
):
    chans, rows, cols = x_in.shape
    states = decay_rate.shape[2]
    height = rows * n
    f32, bf16 = jnp.float32, jnp.bfloat16
    scratch = [
        pltpu.VMEM((rows + 2, cols + 16, chans), f32),
        pltpu.VMEM((2, cols, chans), bf16),
        pltpu.VMEM((n, 16, chans), bf16),
        pltpu.VMEM((n, 16, chans), bf16),
        pltpu.VMEM((height + 2, 8, chans), f32),
        pltpu.VMEM((rows, cols, chans), f32),
        pltpu.VMEM((512, chans), f32),
        pltpu.VMEM((2, chans, 256), bf16),
        pltpu.VMEM((512, chans), f32),
        pltpu.VMEM((states // 2, 8, chans), f32),
        pltpu.VMEM((states, 8, chans), f32),
        pltpu.VMEM((cols, 8, chans), f32),
        pltpu.VMEM((cols, 8, chans), f32),
        pltpu.VMEM((cols, 8, 128), f32),
        pltpu.VMEM((chans // 128, cols * 8, 128), f32),
        pltpu.VMEM((chans // 128, cols * 8, 128), f32),
        pltpu.VMEM((states // 2, 8, chans), f32),
        pltpu.VMEM((height, 8, chans), f32),
        pltpu.VMEM((height, 8, chans), f32),
        pltpu.VMEM((height, 8, 128), f32),
        pltpu.VMEM((chans // 128, height * 8, 128), f32),
        pltpu.VMEM((chans // 128, height * 8, 128), f32),
        pltpu.VMEM((n, 16, 128), bf16),
        pltpu.VMEM((n, 16, 128), bf16),
        pltpu.SemaphoreType.DMA((2,)),
        pltpu.SemaphoreType.DMA((2,)),
        pltpu.SemaphoreType.DMA((n,)),
        pltpu.SemaphoreType.DMA((n,)),
        pltpu.SemaphoreType.DMA((n,)),
        pltpu.SemaphoreType.DMA((n,)),
    ]
    normed = pl.pallas_call(
        functools.partial(fused_kernel, n),
        out_shape=jax.ShapeDtypeStruct((rows, cols, chans), f32),
        in_specs=[pl.BlockSpec(memory_space=pltpu.VMEM)] * 10,
        out_specs=pl.BlockSpec(memory_space=pltpu.VMEM),
        scratch_shapes=scratch,
        compiler_params=pltpu.CompilerParams(
            collective_id=0, has_side_effects=True, vmem_limit_bytes=40 * 1024 * 1024
        ),
    )(
        x_in.transpose(1, 2, 0),
        conv_weight.T,
        conv_bias[None, :],
        proj_weight,
        dt_weight.transpose(0, 2, 1),
        dt_bias,
        decay_rate.transpose(0, 2, 1),
        skip_gain,
        norm_gain[None, :],
        norm_bias[None, :],
    )
    gate = jax.nn.silu(gate_in.astype(f32))
    return (normed.transpose(2, 0, 1) * gate).astype(bf16)


def on_device(*args):
    n = lax.axis_size("sp")
    chans, rows, cols = args[0].shape
    rank, states = args[5].shape[2], args[7].shape[2]
    fits = (chans, rows, cols, rank, states) == (256, 2, 4 * n, 8, 16)
    if lax.axis_size("ch") == 1 and fits:
        return fused_device(n, *args)
    return plain_device(*args)


def solution(mesh):
    placed = (
        P("ch", "sp", None),
        P("ch", "sp", None),
        P("ch", None),
        P("ch"),
        P(None, None, "ch"),
        P(None, "ch", None),
        P(None, "ch"),
        P(None, "ch", None),
        P(None, "ch"),
        P("ch"),
        P("ch"),
    )
    return jax.shard_map(
        on_device, mesh=mesh, in_specs=placed, out_specs=P("ch", "sp", None), check_vma=False
    )
```

```python
import functools

import jax
import jax.numpy as jnp
from jax import lax
from jax.experimental import pallas as pl
from jax.experimental.pallas import tpu as pltpu
from jax.sharding import PartitionSpec as P

SPAN = 64
MESH = pl.DeviceIdType.MESH
UNROLL = 8
BEFORE = 64


def with_halo(value, sides, width):
    for axis, dim in sides:
        peers, length = (lax.axis_size(axis), value.shape[dim])
        up = [(i, (i + 1) % peers) for i in range(peers - 1)]
        down = [(j, i) for i, j in up]
        last = lax.slice_in_dim(value, length - width, length, axis=dim)
        first = lax.slice_in_dim(value, 0, width, axis=dim)
        before = lax.ppermute(last, axis, up)
        after = lax.ppermute(first, axis, down)
        value = jnp.concatenate([before, value, after], axis=dim)
    return value


def conv_silu(padded, conv_weight, conv_bias, rows, cols):
    total = jnp.zeros((padded.shape[0], rows, cols), jnp.float32) + conv_bias[:, None, None]
    for offset in range(9):
        down_shift = offset // 3
        side_shift = offset % 3
        window = padded[:, down_shift : down_shift + rows, side_shift : side_shift + cols].astype(
            jnp.float32
        )
        total = total + conv_weight[:, offset][:, None, None] * window
    return jax.nn.silu(total).astype(jnp.bfloat16)


def steps_first(low_rank, dt_weight, dt_bias):
    length, rank, lines = low_rank.shape
    total = jnp.zeros((length, dt_weight.shape[0], lines), jnp.float32) + dt_bias[None, :, None]
    for rank_index in range(rank):
        total = (
            total
            + dt_weight[:, rank_index][None, :, None]
            * low_rank[:, rank_index].astype(jnp.float32)[:, None, :]
        )
    return jax.nn.softplus(total)


def block_scan(values, low_rank, b_coef, c_coef, dt_weight, dt_bias, rates, skip_gain, reverse):
    length, chans, lines = values.shape
    states = rates.shape[1]
    block_len = min(SPAN, length)
    count = length // block_len
    deltas = steps_first(low_rank, dt_weight, dt_bias)
    rates_turned = rates.T[:, :, None]
    skip_column = skip_gain[:, None]

    def single(state, items):
        value_now, delta_now, b_now, c_now = items
        values_now = value_now.astype(jnp.float32)
        decays = jnp.exp(-delta_now[None] * rates_turned)
        state = (
            decays * state + (delta_now * values_now)[None] * b_now.astype(jnp.float32)[:, None, :]
        )
        output = (
            jnp.sum(c_now.astype(jnp.float32)[:, None, :] * state, axis=0)
            + skip_column * values_now
        )
        return (state, output)

    def advance(state, block_items):
        return lax.scan(single, state, block_items, reverse=reverse, unroll=block_len)

    items = (
        values.reshape(count, block_len, chans, lines),
        deltas.reshape(count, block_len, chans, lines),
        b_coef.reshape(count, block_len, states, lines),
        c_coef.reshape(count, block_len, states, lines),
    )
    initial = jnp.zeros((states, chans, lines), jnp.float32)
    _, outputs = lax.scan(advance, initial, items, reverse=reverse)
    return outputs.reshape(length, chans, lines)


def two_directions(values, proj_pair, dt_weight, dt_bias, decay_rate, skip_gain, first):
    rank = dt_weight.shape[2]
    states = decay_rate.shape[2]
    total = jnp.zeros(values.shape, jnp.float32)
    for offset in range(2):
        direction = first + offset
        block = proj_pair[offset]
        total = total + block_scan(
            values,
            block[:, :rank],
            block[:, rank : rank + states],
            block[:, rank + states :],
            dt_weight[direction],
            dt_bias[direction],
            decay_rate[direction],
            skip_gain[direction],
            offset == 1,
        )
    return total


def plain_device(
    x_in,
    gate_in,
    conv_weight,
    conv_bias,
    proj_weight,
    dt_weight,
    dt_bias,
    decay_rate,
    skip_gain,
    norm_gain,
    norm_bias,
):
    chans, rows, cols = x_in.shape
    rank = dt_weight.shape[2]
    states = decay_rate.shape[2]
    width_proj = rank + 2 * states
    padded = with_halo(x_in, (("sp", 1),), 1)
    padded = jnp.pad(padded, ((0, 0), (0, 0), (1, 1)))
    conv_out = conv_silu(padded, conv_weight, conv_bias, rows, cols)
    flattened = conv_out.reshape(chans, rows * cols)
    partial_sum = jnp.dot(
        proj_weight[:2].reshape(2 * width_proj, chans),
        flattened,
        preferred_element_type=jnp.float32,
    )
    row_proj = lax.psum(partial_sum.astype(jnp.bfloat16), "ch").reshape(2, width_proj, rows, cols)
    col_in = lax.all_to_all(conv_out, "sp", split_axis=2, concat_axis=1, tiled=True)
    col_flat = col_in.reshape(chans, col_in.shape[1] * col_in.shape[2])
    col_partial = jnp.dot(
        proj_weight[2:].reshape(2 * width_proj, chans), col_flat, preferred_element_type=jnp.float32
    )
    col_proj = lax.psum(col_partial.astype(jnp.bfloat16), "ch").reshape(
        2, width_proj, col_in.shape[1], col_in.shape[2]
    )
    row_values = conv_out.transpose(2, 0, 1)
    row_pair = row_proj.transpose(0, 3, 1, 2)
    horizontal = two_directions(
        row_values, row_pair, dt_weight, dt_bias, decay_rate, skip_gain, 0
    ).transpose(1, 2, 0)
    col_values = col_in.transpose(1, 0, 2)
    col_pair = col_proj.transpose(0, 2, 1, 3)
    vertical = two_directions(col_values, col_pair, dt_weight, dt_bias, decay_rate, skip_gain, 2)
    vertical = vertical.transpose(1, 0, 2).astype(jnp.bfloat16)
    vertical_rows = lax.all_to_all(vertical, "sp", split_axis=1, concat_axis=2, tiled=True)
    combined = horizontal + vertical_rows.astype(jnp.float32)
    sum_first, sum_second = lax.psum(
        (jnp.sum(combined, axis=0), jnp.sum(combined * combined, axis=0)), "ch"
    )
    chans_total = chans * lax.axis_size("ch")
    mean = sum_first / chans_total
    var = sum_second / chans_total - mean * mean
    normed = (combined - mean[None]) * lax.rsqrt(var[None] + 1e-05) * norm_gain[
        :, None, None
    ] + norm_bias[:, None, None]
    return (normed * jax.nn.silu(gate_in.astype(jnp.float32))).astype(jnp.bfloat16)


def fused_kernel(
    n,
    x_ref,
    cw_ref,
    cb_ref,
    pw_ref,
    dw_ref,
    db_ref,
    rate_ref,
    skip_ref,
    gain_ref,
    nbias_ref,
    out_ref,
    xs,
    xt,
    normed,
    xpad,
    halo,
    xsend,
    xrecv,
    xv,
    cr,
    wf,
    wt,
    wd,
    rate_h,
    rate_v,
    u_h,
    d_h,
    p_h,
    ya_h,
    yb_h,
    state_h,
    u_v,
    d_v,
    p_v,
    ya_v,
    yb_v,
    vsend,
    vrecv,
    halo_send,
    halo_recv,
    xs_sem,
    xr_sem,
    vs_sem,
    vr_sem,
):
    rows, cols, chans = cr.shape
    height = rows * n
    rank = dw_ref.shape[1]
    states = rate_ref.shape[1]
    width = rank + 2 * states
    half = states // 2
    f32, bf16 = jnp.float32, jnp.bfloat16
    me = lax.axis_index("sp")
    right, left = lax.rem(me + 1, n), lax.rem(me + n - 1, n)

    barrier = pltpu.get_barrier_semaphore()

    @pl.loop(1, n)
    def _(d):
        pl.semaphore_signal(
            barrier, inc=1, device_id={"sp": lax.rem(me + d, n)}, device_id_type=MESH
        )

    low4_one = lax.broadcasted_iota(jnp.int32, (8, 128), 0) < 4
    low6 = lax.broadcasted_iota(jnp.int32, (8, chans), 0) < 6

    edge = jnp.zeros((rows + 2, 8, chans), f32)
    xpad[:, 0:8, :] = edge
    xpad[:, cols + 8 : cols + 16, :] = edge
    xs[...] = x_ref[...].astype(f32)
    for r in range(rows):
        upright = xs[pl.ds(r, chans, stride=rows), :].T
        xpad[r + 1, 8 : cols + 8, :] = upright
        xt[r] = upright.astype(bf16)
    for j in range(n):
        at = 8 + 4 * j - 1
        first, second = xpad[1, at : at + 8, :], xpad[2, at : at + 8, :]
        lower = jnp.where(low6, first, pltpu.roll(second, 6, 0))
        rest = pltpu.roll(second, 6, 0)
        near, far = rest[:, 0:128], pltpu.roll(rest[:, 128:256], 4, 0)
        xsend[j] = jnp.concatenate(
            [lower[:, 0:128], lower[:, 128:256], jnp.where(low4_one, near, far)], axis=0
        ).astype(bf16)
    xrecv[pl.ds(me, 1)] = xsend[pl.ds(me, 1)]

    pl.semaphore_wait(barrier, n - 1)

    def halo_copy(which):
        return pltpu.make_async_remote_copy(
            src_ref=xt.at[rows - 1 if which == 0 else 0],
            dst_ref=halo.at[which],
            send_sem=halo_send.at[which],
            recv_sem=halo_recv.at[which],
            device_id={"sp": right if which == 0 else left},
            device_id_type=MESH,
        )

    halo_copy(0).start()
    halo_copy(1).start()

    def x_copy(d, slot):
        dst = lax.rem(me + d, n)
        return pltpu.make_async_remote_copy(
            src_ref=xsend.at[dst],
            dst_ref=xrecv.at[slot],
            send_sem=xs_sem.at[d],
            recv_sem=xr_sem.at[d],
            device_id={"sp": dst},
            device_id_type=MESH,
        )

    def v_copy(dst, slot):
        return pltpu.make_async_remote_copy(
            src_ref=vsend.at[dst],
            dst_ref=vrecv.at[slot],
            send_sem=vs_sem.at[dst],
            recv_sem=vr_sem.at[slot],
            device_id={"sp": dst},
            device_id_type=MESH,
        )

    @pl.loop(1, n)
    def _(d):
        x_copy(d, me).start()

    sub = lax.broadcasted_iota(jnp.int32, (8, chans), 0)
    low4 = sub < 4
    low2 = sub < 2
    dir_h = (sub // 2) % 2 == 0
    dir_v = low4
    wf[...] = jnp.zeros(wf.shape, f32)
    wd[...] = jnp.zeros(wd.shape, f32)
    for k in range(4):
        base = 128 * k
        rowsw = pw_ref[k].astype(f32)
        wf[base : base + width, :] = rowsw
        wf[base + width : base + width + rank, :] = rowsw[0:rank]
        full = dw_ref[k]
        high = full.astype(bf16).astype(f32)
        wd[base : base + rank, :] = high
        wd[base + width : base + width + rank, :] = full - high
    for first in range(2):
        wt[first] = wf[256 * first : 256 * first + 256, :].T.astype(bf16)
    for s in range(states):
        rate_v[s] = -jnp.where(
            dir_v, rate_ref[2, s : s + 1, :], rate_ref[3, s : s + 1, :]
        )
    for s in range(half):
        lower = jnp.where(dir_h, rate_ref[0, s : s + 1, :], rate_ref[1, s : s + 1, :])
        upper = jnp.where(
            dir_h, rate_ref[0, s + half : s + half + 1, :], rate_ref[1, s + half : s + half + 1, :]
        )
        rate_h[s] = -jnp.where(low4, lower, upper)

    def prepare(steps, first, dirs, u, dl, p, halves):
        weights = wt[first]
        up = wd[256 * first : 256 * first + 256, :].astype(bf16)
        bias = jnp.where(dirs, db_ref[2 * first : 2 * first + 1], db_ref[2 * first + 1 : 2 * first + 2])
        bias = bias[None]
        pick = dirs[:, 0:128][None]
        lift = low4_one[None]
        size = 32

        @pl.loop(0, steps // size)
        def _(i):
            at = pl.ds(i * size, size)
            flat = u[at].reshape(size * 8, chans).astype(bf16)
            proj = lax.dot_general(
                flat, weights, (((1,), (0,)), ((), ())), preferred_element_type=f32
            )
            proj = proj.astype(bf16).astype(f32).reshape(size, 8, 256)
            one, two = proj[:, :, 0:128], proj[:, :, 128:256]
            own = jnp.where(pick, one, two)
            both = jnp.concatenate(
                [jnp.where(pick, one, 0.0), jnp.where(pick, 0.0, two)], axis=2
            )
            pre = jnp.dot(
                both.reshape(size * 8, 256).astype(bf16), up, preferred_element_type=f32
            ).reshape(size, 8, chans)
            pre = pre + bias
            dl[at] = jnp.maximum(pre, 0.0) + jnp.log(1.0 + jnp.exp(-jnp.abs(pre)))
            if halves:
                own = jnp.where(lift, own, pltpu.roll(own, 128 - half, 2))
            p[at] = own

    def step(t, state, u, dl, p, rate, ya, yb, last, count, offset):
        delta, tile = dl[t], p[t]
        drive = delta * u[t]
        total = None
        new = []
        for s in range(count):
            decay = jnp.exp(delta * rate[s])
            b_now = jnp.broadcast_to(tile[:, rank + s : rank + s + 1], (8, chans))
            c_now = jnp.broadcast_to(tile[:, offset + s : offset + s + 1], (8, chans))
            now = decay * state[s] + drive * b_now
            new.append(now)
            term = c_now * now
            total = term if total is None else total + term
        for k in range(chans // 128):
            piece = total[:, k * 128 : k * 128 + 128]
            ya[k, pl.ds(pl.multiple_of(t * 8, 8), 8), :] = piece
            yb[k, pl.ds(pl.multiple_of((last - t) * 8, 8), 8), :] = piece
        return tuple(new)

    for which in range(2):
        halo_copy(which).wait()
    above, below = halo[0].astype(f32), halo[1].astype(f32)
    xpad[0, 8 : cols + 8, :] = jnp.where(me == 0, jnp.zeros_like(above), above)
    xpad[rows + 1, 8 : cols + 8, :] = jnp.where(me == n - 1, jnp.zeros_like(below), below)
    block = 32
    for r in range(rows):
        for c in range(0, cols, block):
            total = jnp.zeros((block, chans), f32) + cb_ref[...]
            for i in range(3):
                for j in range(3):
                    window = xpad[r + i, 7 + c + j : 7 + c + j + block, :]
                    total = total + cw_ref[3 * i + j : 3 * i + j + 1, :] * window
            cr[r, c : c + block, :] = jax.nn.silu(total).astype(bf16).astype(f32)

    odd = sub % 2 == 1

    def spread(t):
        ahead = jnp.where(odd, cr[1, pl.ds(t, 1), :], cr[0, pl.ds(t, 1), :])
        back = jnp.where(odd, cr[1, pl.ds(cols - 1 - t, 1), :], cr[0, pl.ds(cols - 1 - t, 1), :])
        u_h[t] = jnp.where(dir_h, ahead, back)

    @pl.loop(0, cols // 8)
    def _(i):
        for k in range(8):
            spread(i * 8 + k)

    prepare(cols, 0, dir_h, u_h, d_h, p_h, True)

    def row_steps(lower, upper, state):
        def body(t, state):
            return step(
                t, state, u_h, d_h, p_h, rate_h, ya_h, yb_h, cols - 1, half, rank + states
            )

        return lax.fori_loop(lower, upper, body, state, unroll=UNROLL)

    state = row_steps(0, BEFORE, tuple(jnp.zeros((8, chans), f32) for _ in range(half)))
    for s in range(half):
        state_h[s] = state[s]

    @pl.loop(1, n)
    def _(d):
        x_copy(d, lax.rem(me + n - d, n)).wait()

    nothing = jnp.zeros((8, chans), f32)
    xv[0] = nothing
    xv[height + 1] = nothing

    @pl.loop(0, n)
    def _(j):
        tiles = xrecv[j].astype(f32)
        rest = tiles[16:24]
        lower = jnp.concatenate([tiles[0:8], tiles[8:16]], axis=1)
        rest = jnp.concatenate([rest, pltpu.roll(rest, 4, 0)], axis=1)
        xv[1 + 2 * j] = lower
        xv[2 + 2 * j] = jnp.where(low2, pltpu.roll(lower, 2, 0), pltpu.roll(rest, 2, 0))

    def conv_step(t):
        total = jnp.zeros((8, chans), f32) + cb_ref[...]
        tiles = [xv[t], xv[t + 1], xv[t + 2]]
        for j in range(3):
            part = None
            for i in range(3):
                term = cw_ref[3 * i + j : 3 * i + j + 1, :] * tiles[i]
                part = term if part is None else part + term
            total = total + pltpu.roll(part, (8 - j) % 8, 0)
        value = jax.nn.silu(total).astype(bf16).astype(f32)
        turned = pltpu.roll(value, 4, 0)
        u_v[t, 0:4, :] = value[0:4]
        u_v[height - 1 - t, 4:8, :] = turned[4:8]

    @pl.loop(0, height // 8)
    def _(i):
        for k in range(8):
            conv_step(i * 8 + k)

    prepare(height, 1, dir_v, u_v, d_v, p_v, False)

    def col_body(t, state):
        return step(
            t, state, u_v, d_v, p_v, rate_v, ya_v, yb_v, height - 1, states, rank + states
        )

    state = lax.fori_loop(
        0, height // 2, col_body, tuple(jnp.zeros((8, chans), f32) for _ in range(states)), unroll=UNROLL
    )

    skip_v = skip_ref[2:3, :] + skip_ref[3:4, :]

    def column_row(t):
        at = pl.ds(pl.multiple_of(t * 8, 8), 8)
        parts = [
            ya_v[k, at, :] + pltpu.roll(yb_v[k, at, :], 4, 0) for k in range(chans // 128)
        ]
        return jnp.concatenate(parts, axis=1) + skip_v * u_v[t]

    def column_tile(j):
        tile = jnp.where(low4, column_row(2 * j), pltpu.roll(column_row(2 * j + 1), 4, 0))
        return jnp.concatenate([tile[:, 0:128], tile[:, 128:256]], axis=0).astype(bf16)

    def col_part(c, state):
        for k in range(8):
            state = col_body(height // 2 + 8 * c + k, state)
        for k in range(4):
            for j in (n // 2 - 4 - 4 * c + k, n // 2 + 4 * c + k):
                vsend[j] = column_tile(j)

                @pl.when(j != me)
                def _():
                    v_copy(j, me).start()

        return state

    lax.fori_loop(0, height // 16, col_part, state)

    vrecv[pl.ds(me, 1)] = vsend[pl.ds(me, 1)]

    row_steps(BEFORE, cols, tuple(state_h[s] for s in range(half)))

    @pl.loop(1, n)
    def _(d):
        other = lax.rem(me + d, n)
        v_copy(other, other).wait()

    skip_h = skip_ref[0:1, :] + skip_ref[1:2, :]

    def finish(p):
        even, other = vrecv[2 * p].astype(f32), vrecv[2 * p + 1].astype(f32)
        even = jnp.concatenate([even[0:8], even[8:16]], axis=1)
        other = jnp.concatenate([other[0:8], other[8:16]], axis=1)
        at = pl.ds(pl.multiple_of(p * 8, 8), 8)
        for r in range(rows):
            if r == 0:
                upright = jnp.where(low4, even, pltpu.roll(other, 4, 0))
            else:
                upright = jnp.where(low4, pltpu.roll(even, 4, 0), other)
            flat = skip_h * cr[r, at, :]
            for source, line in ((ya_h, r), (ya_h, 4 + r), (yb_h, 2 + r), (yb_h, 6 + r)):
                parts = [
                    source[k, pl.ds(p * 64 + line, 8, stride=8), :]
                    for k in range(chans // 128)
                ]
                flat = flat + jnp.concatenate(parts, axis=1)
            combined = flat + upright
            mean = jnp.sum(combined, axis=1, keepdims=True) / chans
            var = jnp.sum(combined * combined, axis=1, keepdims=True) / chans - mean * mean
            scaled = (combined - mean) * lax.rsqrt(var + 1e-05)
            normed[r, at, :] = scaled * gain_ref[...] + nbias_ref[...]

    @pl.loop(0, cols // 32)
    def _(i):
        for k in range(4):
            finish(4 * i + k)

    for r in range(rows):
        out_ref[pl.ds(r, chans, stride=rows), :] = normed[r].T


def fused_device(
    n,
    x_in,
    gate_in,
    conv_weight,
    conv_bias,
    proj_weight,
    dt_weight,
    dt_bias,
    decay_rate,
    skip_gain,
    norm_gain,
    norm_bias,
):
    chans, rows, cols = x_in.shape
    states = decay_rate.shape[2]
    height = rows * n
    f32, bf16 = jnp.float32, jnp.bfloat16
    scratch = [
        pltpu.VMEM((chans * rows, cols), f32),
        pltpu.VMEM((rows, cols, chans), bf16),
        pltpu.VMEM((rows, cols, chans), f32),
        pltpu.VMEM((rows + 2, cols + 16, chans), f32),
        pltpu.VMEM((2, cols, chans), bf16),
        pltpu.VMEM((n, 24, 128), bf16),
        pltpu.VMEM((n, 24, 128), bf16),
        pltpu.VMEM((height + 2, 8, chans), f32),
        pltpu.VMEM((rows, cols, chans), f32),
        pltpu.VMEM((512, chans), f32),
        pltpu.VMEM((2, chans, 256), bf16),
        pltpu.VMEM((512, chans), f32),
        pltpu.VMEM((states // 2, 8, chans), f32),
        pltpu.VMEM((states, 8, chans), f32),
        pltpu.VMEM((cols, 8, chans), f32),
        pltpu.VMEM((cols, 8, chans), f32),
        pltpu.VMEM((cols, 8, 128), f32),
        pltpu.VMEM((chans // 128, cols * 8, 128), f32),
        pltpu.VMEM((chans // 128, cols * 8, 128), f32),
        pltpu.VMEM((states // 2, 8, chans), f32),
        pltpu.VMEM((height, 8, chans), f32),
        pltpu.VMEM((height, 8, chans), f32),
        pltpu.VMEM((height, 8, 128), f32),
        pltpu.VMEM((chans // 128, height * 8, 128), f32),
        pltpu.VMEM((chans // 128, height * 8, 128), f32),
        pltpu.VMEM((n, 16, 128), bf16),
        pltpu.VMEM((n, 16, 128), bf16),
        pltpu.SemaphoreType.DMA((2,)),
        pltpu.SemaphoreType.DMA((2,)),
        pltpu.SemaphoreType.DMA((n,)),
        pltpu.SemaphoreType.DMA((n,)),
        pltpu.SemaphoreType.DMA((n,)),
        pltpu.SemaphoreType.DMA((n,)),
    ]
    normed = pl.pallas_call(
        functools.partial(fused_kernel, n),
        out_shape=jax.ShapeDtypeStruct((chans * rows, cols), f32),
        in_specs=[pl.BlockSpec(memory_space=pltpu.VMEM)] * 10,
        out_specs=pl.BlockSpec(memory_space=pltpu.VMEM),
        scratch_shapes=scratch,
        compiler_params=pltpu.CompilerParams(
            collective_id=0, has_side_effects=True, vmem_limit_bytes=40 * 1024 * 1024
        ),
    )(
        x_in.reshape(chans * rows, cols),
        conv_weight.T,
        conv_bias[None, :],
        proj_weight,
        dt_weight.transpose(0, 2, 1),
        dt_bias,
        decay_rate.transpose(0, 2, 1),
        skip_gain,
        norm_gain[None, :],
        norm_bias[None, :],
    )
    gate = jax.nn.silu(gate_in.astype(f32))
    return (normed.reshape(chans, rows, cols) * gate).astype(bf16)


def on_device(*args):
    n = lax.axis_size("sp")
    chans, rows, cols = args[0].shape
    rank, states = args[5].shape[2], args[7].shape[2]
    fits = (chans, rows, cols, rank, states) == (256, 2, 4 * n, 8, 16)
    if lax.axis_size("ch") == 1 and fits:
        return fused_device(n, *args)
    return plain_device(*args)


def solution(mesh):
    placed = (
        P("ch", "sp", None),
        P("ch", "sp", None),
        P("ch", None),
        P("ch"),
        P(None, None, "ch"),
        P(None, "ch", None),
        P(None, "ch"),
        P(None, "ch", None),
        P(None, "ch"),
        P("ch"),
        P("ch"),
    )
    return jax.shard_map(
        on_device, mesh=mesh, in_specs=placed, out_specs=P("ch", "sp", None), check_vma=False
    )
```

```python
import functools

import jax
import jax.numpy as jnp
from jax import lax
from jax.experimental import pallas as pl
from jax.experimental.pallas import tpu as pltpu
from jax.sharding import PartitionSpec as P

SPAN = 64
MESH = pl.DeviceIdType.MESH
UNROLL = 8
BEFORE = 64


def with_halo(value, sides, width):
    for axis, dim in sides:
        peers, length = (lax.axis_size(axis), value.shape[dim])
        up = [(i, (i + 1) % peers) for i in range(peers - 1)]
        down = [(j, i) for i, j in up]
        last = lax.slice_in_dim(value, length - width, length, axis=dim)
        first = lax.slice_in_dim(value, 0, width, axis=dim)
        before = lax.ppermute(last, axis, up)
        after = lax.ppermute(first, axis, down)
        value = jnp.concatenate([before, value, after], axis=dim)
    return value


def conv_silu(padded, conv_weight, conv_bias, rows, cols):
    total = jnp.zeros((padded.shape[0], rows, cols), jnp.float32) + conv_bias[:, None, None]
    for offset in range(9):
        down_shift = offset // 3
        side_shift = offset % 3
        window = padded[:, down_shift : down_shift + rows, side_shift : side_shift + cols].astype(
            jnp.float32
        )
        total = total + conv_weight[:, offset][:, None, None] * window
    return jax.nn.silu(total).astype(jnp.bfloat16)


def steps_first(low_rank, dt_weight, dt_bias):
    length, rank, lines = low_rank.shape
    total = jnp.zeros((length, dt_weight.shape[0], lines), jnp.float32) + dt_bias[None, :, None]
    for rank_index in range(rank):
        total = (
            total
            + dt_weight[:, rank_index][None, :, None]
            * low_rank[:, rank_index].astype(jnp.float32)[:, None, :]
        )
    return jax.nn.softplus(total)


def block_scan(values, low_rank, b_coef, c_coef, dt_weight, dt_bias, rates, skip_gain, reverse):
    length, chans, lines = values.shape
    states = rates.shape[1]
    block_len = min(SPAN, length)
    count = length // block_len
    deltas = steps_first(low_rank, dt_weight, dt_bias)
    rates_turned = rates.T[:, :, None]
    skip_column = skip_gain[:, None]

    def single(state, items):
        value_now, delta_now, b_now, c_now = items
        values_now = value_now.astype(jnp.float32)
        decays = jnp.exp(-delta_now[None] * rates_turned)
        state = (
            decays * state + (delta_now * values_now)[None] * b_now.astype(jnp.float32)[:, None, :]
        )
        output = (
            jnp.sum(c_now.astype(jnp.float32)[:, None, :] * state, axis=0)
            + skip_column * values_now
        )
        return (state, output)

    def advance(state, block_items):
        return lax.scan(single, state, block_items, reverse=reverse, unroll=block_len)

    items = (
        values.reshape(count, block_len, chans, lines),
        deltas.reshape(count, block_len, chans, lines),
        b_coef.reshape(count, block_len, states, lines),
        c_coef.reshape(count, block_len, states, lines),
    )
    initial = jnp.zeros((states, chans, lines), jnp.float32)
    _, outputs = lax.scan(advance, initial, items, reverse=reverse)
    return outputs.reshape(length, chans, lines)


def two_directions(values, proj_pair, dt_weight, dt_bias, decay_rate, skip_gain, first):
    rank = dt_weight.shape[2]
    states = decay_rate.shape[2]
    total = jnp.zeros(values.shape, jnp.float32)
    for offset in range(2):
        direction = first + offset
        block = proj_pair[offset]
        total = total + block_scan(
            values,
            block[:, :rank],
            block[:, rank : rank + states],
            block[:, rank + states :],
            dt_weight[direction],
            dt_bias[direction],
            decay_rate[direction],
            skip_gain[direction],
            offset == 1,
        )
    return total


def plain_device(
    x_in,
    gate_in,
    conv_weight,
    conv_bias,
    proj_weight,
    dt_weight,
    dt_bias,
    decay_rate,
    skip_gain,
    norm_gain,
    norm_bias,
):
    chans, rows, cols = x_in.shape
    rank = dt_weight.shape[2]
    states = decay_rate.shape[2]
    width_proj = rank + 2 * states
    padded = with_halo(x_in, (("sp", 1),), 1)
    padded = jnp.pad(padded, ((0, 0), (0, 0), (1, 1)))
    conv_out = conv_silu(padded, conv_weight, conv_bias, rows, cols)
    flattened = conv_out.reshape(chans, rows * cols)
    partial_sum = jnp.dot(
        proj_weight[:2].reshape(2 * width_proj, chans),
        flattened,
        preferred_element_type=jnp.float32,
    )
    row_proj = lax.psum(partial_sum.astype(jnp.bfloat16), "ch").reshape(2, width_proj, rows, cols)
    col_in = lax.all_to_all(conv_out, "sp", split_axis=2, concat_axis=1, tiled=True)
    col_flat = col_in.reshape(chans, col_in.shape[1] * col_in.shape[2])
    col_partial = jnp.dot(
        proj_weight[2:].reshape(2 * width_proj, chans), col_flat, preferred_element_type=jnp.float32
    )
    col_proj = lax.psum(col_partial.astype(jnp.bfloat16), "ch").reshape(
        2, width_proj, col_in.shape[1], col_in.shape[2]
    )
    row_values = conv_out.transpose(2, 0, 1)
    row_pair = row_proj.transpose(0, 3, 1, 2)
    horizontal = two_directions(
        row_values, row_pair, dt_weight, dt_bias, decay_rate, skip_gain, 0
    ).transpose(1, 2, 0)
    col_values = col_in.transpose(1, 0, 2)
    col_pair = col_proj.transpose(0, 2, 1, 3)
    vertical = two_directions(col_values, col_pair, dt_weight, dt_bias, decay_rate, skip_gain, 2)
    vertical = vertical.transpose(1, 0, 2).astype(jnp.bfloat16)
    vertical_rows = lax.all_to_all(vertical, "sp", split_axis=1, concat_axis=2, tiled=True)
    combined = horizontal + vertical_rows.astype(jnp.float32)
    sum_first, sum_second = lax.psum(
        (jnp.sum(combined, axis=0), jnp.sum(combined * combined, axis=0)), "ch"
    )
    chans_total = chans * lax.axis_size("ch")
    mean = sum_first / chans_total
    var = sum_second / chans_total - mean * mean
    normed = (combined - mean[None]) * lax.rsqrt(var[None] + 1e-05) * norm_gain[
        :, None, None
    ] + norm_bias[:, None, None]
    return (normed * jax.nn.silu(gate_in.astype(jnp.float32))).astype(jnp.bfloat16)


def fused_kernel(n, *refs):
    sources, out_ref, held = refs[:10], refs[10], refs[11:21]
    (
        x_ref,
        cw_ref,
        cb_ref,
        pw_ref,
        dw_ref,
        db_ref,
        rate_ref,
        skip_ref,
        gain_ref,
        nbias_ref,
    ) = held
    (
        xs,
        xt,
        normed,
        xpad,
        halo,
        xsend,
        xrecv,
        xv,
        cr,
        wf,
        wt,
        wd,
        rate_h,
        rate_v,
        u_h,
        d_h,
        p_h,
        ya_h,
        yb_h,
        state_h,
        u_v,
        d_v,
        p_v,
        ya_v,
        yb_v,
        vsend,
        vrecv,
        halo_send,
        halo_recv,
        xs_sem,
        xr_sem,
        vs_sem,
        vr_sem,
        in_sem,
    ) = refs[21:]
    rows, cols, chans = cr.shape
    height = rows * n
    rank = dw_ref.shape[1]
    states = rate_ref.shape[1]
    width = rank + 2 * states
    half = states // 2
    f32, bf16 = jnp.float32, jnp.bfloat16
    me = lax.axis_index("sp")
    right, left = lax.rem(me + 1, n), lax.rem(me + n - 1, n)

    loads = [
        pltpu.make_async_copy(source, target, in_sem.at[i])
        for i, (source, target) in enumerate(zip(sources, held))
    ]
    for load in loads:
        load.start()

    barrier = pltpu.get_barrier_semaphore()

    @pl.loop(1, n)
    def _(d):
        pl.semaphore_signal(
            barrier, inc=1, device_id={"sp": lax.rem(me + d, n)}, device_id_type=MESH
        )

    low4_one = lax.broadcasted_iota(jnp.int32, (8, 128), 0) < 4
    low6 = lax.broadcasted_iota(jnp.int32, (8, chans), 0) < 6

    edge = jnp.zeros((rows + 2, 8, chans), f32)
    xpad[:, 0:8, :] = edge
    xpad[:, cols + 8 : cols + 16, :] = edge
    loads[0].wait()
    xs[...] = x_ref[...].astype(f32)
    for r in range(rows):
        upright = xs[pl.ds(r, chans, stride=rows), :].T
        xpad[r + 1, 8 : cols + 8, :] = upright
        xt[r] = upright.astype(bf16)
    for j in range(n):
        at = 8 + 4 * j - 1
        first, second = xpad[1, at : at + 8, :], xpad[2, at : at + 8, :]
        lower = jnp.where(low6, first, pltpu.roll(second, 6, 0))
        rest = pltpu.roll(second, 6, 0)
        near, far = rest[:, 0:128], pltpu.roll(rest[:, 128:256], 4, 0)
        xsend[j] = jnp.concatenate(
            [lower[:, 0:128], lower[:, 128:256], jnp.where(low4_one, near, far)], axis=0
        ).astype(bf16)
    xrecv[pl.ds(me, 1)] = xsend[pl.ds(me, 1)]

    pl.semaphore_wait(barrier, n - 1)

    def halo_copy(which):
        return pltpu.make_async_remote_copy(
            src_ref=xt.at[rows - 1 if which == 0 else 0],
            dst_ref=halo.at[which],
            send_sem=halo_send.at[which],
            recv_sem=halo_recv.at[which],
            device_id={"sp": right if which == 0 else left},
            device_id_type=MESH,
        )

    halo_copy(0).start()
    halo_copy(1).start()

    def x_copy(d, slot):
        dst = lax.rem(me + d, n)
        return pltpu.make_async_remote_copy(
            src_ref=xsend.at[dst],
            dst_ref=xrecv.at[slot],
            send_sem=xs_sem.at[d],
            recv_sem=xr_sem.at[d],
            device_id={"sp": dst},
            device_id_type=MESH,
        )

    def v_copy(dst, slot):
        return pltpu.make_async_remote_copy(
            src_ref=vsend.at[dst],
            dst_ref=vrecv.at[slot],
            send_sem=vs_sem.at[dst],
            recv_sem=vr_sem.at[slot],
            device_id={"sp": dst},
            device_id_type=MESH,
        )

    @pl.loop(1, n)
    def _(d):
        x_copy(d, me).start()

    sub = lax.broadcasted_iota(jnp.int32, (8, chans), 0)
    low4 = sub < 4
    low2 = sub < 2
    dir_h = (sub // 2) % 2 == 0
    dir_v = low4
    for load in loads[1:]:
        load.wait()
    wf[...] = jnp.zeros(wf.shape, f32)
    wd[...] = jnp.zeros(wd.shape, f32)
    for k in range(4):
        base = 128 * k
        rowsw = pw_ref[k].astype(f32)
        wf[base : base + width, :] = rowsw
        wf[base + width : base + width + rank, :] = rowsw[0:rank]
        full = dw_ref[k]
        high = full.astype(bf16).astype(f32)
        wd[base : base + rank, :] = high
        wd[base + width : base + width + rank, :] = full - high
    for first in range(2):
        wt[first] = wf[256 * first : 256 * first + 256, :].T.astype(bf16)
    for s in range(states):
        rate_v[s] = -jnp.where(
            dir_v, rate_ref[2, s : s + 1, :], rate_ref[3, s : s + 1, :]
        )
    for s in range(half):
        lower = jnp.where(dir_h, rate_ref[0, s : s + 1, :], rate_ref[1, s : s + 1, :])
        upper = jnp.where(
            dir_h, rate_ref[0, s + half : s + half + 1, :], rate_ref[1, s + half : s + half + 1, :]
        )
        rate_h[s] = -jnp.where(low4, lower, upper)

    def prepare(steps, first, dirs, u, dl, p, halves):
        weights = wt[first]
        up = wd[256 * first : 256 * first + 256, :].astype(bf16)
        bias = jnp.where(dirs, db_ref[2 * first : 2 * first + 1], db_ref[2 * first + 1 : 2 * first + 2])
        bias = bias[None]
        pick = dirs[:, 0:128][None]
        lift = low4_one[None]
        size = 32

        @pl.loop(0, steps // size)
        def _(i):
            at = pl.ds(i * size, size)
            flat = u[at].reshape(size * 8, chans).astype(bf16)
            proj = lax.dot_general(
                flat, weights, (((1,), (0,)), ((), ())), preferred_element_type=f32
            )
            proj = proj.astype(bf16).astype(f32).reshape(size, 8, 256)
            one, two = proj[:, :, 0:128], proj[:, :, 128:256]
            own = jnp.where(pick, one, two)
            both = jnp.concatenate(
                [jnp.where(pick, one, 0.0), jnp.where(pick, 0.0, two)], axis=2
            )
            pre = jnp.dot(
                both.reshape(size * 8, 256).astype(bf16), up, preferred_element_type=f32
            ).reshape(size, 8, chans)
            pre = pre + bias
            dl[at] = jnp.maximum(pre, 0.0) + jnp.log(1.0 + jnp.exp(-jnp.abs(pre)))
            if halves:
                own = jnp.where(lift, own, pltpu.roll(own, 128 - half, 2))
            p[at] = own

    def step(t, state, u, dl, p, rate, ya, yb, last, count, offset):
        delta, tile = dl[t], p[t]
        drive = delta * u[t]
        total = None
        new = []
        for s in range(count):
            decay = jnp.exp(delta * rate[s])
            b_now = jnp.broadcast_to(tile[:, rank + s : rank + s + 1], (8, chans))
            c_now = jnp.broadcast_to(tile[:, offset + s : offset + s + 1], (8, chans))
            now = decay * state[s] + drive * b_now
            new.append(now)
            term = c_now * now
            total = term if total is None else total + term
        for k in range(chans // 128):
            piece = total[:, k * 128 : k * 128 + 128]
            ya[k, pl.ds(pl.multiple_of(t * 8, 8), 8), :] = piece
            yb[k, pl.ds(pl.multiple_of((last - t) * 8, 8), 8), :] = piece
        return tuple(new)

    for which in range(2):
        halo_copy(which).wait()
    above, below = halo[0].astype(f32), halo[1].astype(f32)
    xpad[0, 8 : cols + 8, :] = jnp.where(me == 0, jnp.zeros_like(above), above)
    xpad[rows + 1, 8 : cols + 8, :] = jnp.where(me == n - 1, jnp.zeros_like(below), below)
    block = 32
    for r in range(rows):
        for c in range(0, cols, block):
            total = jnp.zeros((block, chans), f32) + cb_ref[...]
            for i in range(3):
                for j in range(3):
                    window = xpad[r + i, 7 + c + j : 7 + c + j + block, :]
                    total = total + cw_ref[3 * i + j : 3 * i + j + 1, :] * window
            cr[r, c : c + block, :] = jax.nn.silu(total).astype(bf16).astype(f32)

    odd = sub % 2 == 1

    def spread(t):
        ahead = jnp.where(odd, cr[1, pl.ds(t, 1), :], cr[0, pl.ds(t, 1), :])
        back = jnp.where(odd, cr[1, pl.ds(cols - 1 - t, 1), :], cr[0, pl.ds(cols - 1 - t, 1), :])
        u_h[t] = jnp.where(dir_h, ahead, back)

    @pl.loop(0, cols // 8)
    def _(i):
        for k in range(8):
            spread(i * 8 + k)

    prepare(cols, 0, dir_h, u_h, d_h, p_h, True)

    def row_steps(lower, upper, state):
        def body(t, state):
            return step(
                t, state, u_h, d_h, p_h, rate_h, ya_h, yb_h, cols - 1, half, rank + states
            )

        return lax.fori_loop(lower, upper, body, state, unroll=UNROLL)

    state = row_steps(0, BEFORE, tuple(jnp.zeros((8, chans), f32) for _ in range(half)))
    for s in range(half):
        state_h[s] = state[s]

    @pl.loop(1, n)
    def _(d):
        x_copy(d, lax.rem(me + n - d, n)).wait()

    nothing = jnp.zeros((8, chans), f32)
    xv[0] = nothing
    xv[height + 1] = nothing

    @pl.loop(0, n)
    def _(j):
        tiles = xrecv[j].astype(f32)
        rest = tiles[16:24]
        lower = jnp.concatenate([tiles[0:8], tiles[8:16]], axis=1)
        rest = jnp.concatenate([rest, pltpu.roll(rest, 4, 0)], axis=1)
        xv[1 + 2 * j] = lower
        xv[2 + 2 * j] = jnp.where(low2, pltpu.roll(lower, 2, 0), pltpu.roll(rest, 2, 0))

    def conv_step(t):
        total = jnp.zeros((8, chans), f32) + cb_ref[...]
        tiles = [xv[t], xv[t + 1], xv[t + 2]]
        for j in range(3):
            part = None
            for i in range(3):
                term = cw_ref[3 * i + j : 3 * i + j + 1, :] * tiles[i]
                part = term if part is None else part + term
            total = total + pltpu.roll(part, (8 - j) % 8, 0)
        value = jax.nn.silu(total).astype(bf16).astype(f32)
        turned = pltpu.roll(value, 4, 0)
        u_v[t, 0:4, :] = value[0:4]
        u_v[height - 1 - t, 4:8, :] = turned[4:8]

    @pl.loop(0, height // 8)
    def _(i):
        for k in range(8):
            conv_step(i * 8 + k)

    prepare(height, 1, dir_v, u_v, d_v, p_v, False)

    def col_body(t, state):
        return step(
            t, state, u_v, d_v, p_v, rate_v, ya_v, yb_v, height - 1, states, rank + states
        )

    state = lax.fori_loop(
        0, height // 2, col_body, tuple(jnp.zeros((8, chans), f32) for _ in range(states)), unroll=UNROLL
    )

    skip_v = skip_ref[2:3, :] + skip_ref[3:4, :]

    def column_row(t):
        at = pl.ds(pl.multiple_of(t * 8, 8), 8)
        parts = [
            ya_v[k, at, :] + pltpu.roll(yb_v[k, at, :], 4, 0) for k in range(chans // 128)
        ]
        return jnp.concatenate(parts, axis=1) + skip_v * u_v[t]

    def column_tile(j):
        tile = jnp.where(low4, column_row(2 * j), pltpu.roll(column_row(2 * j + 1), 4, 0))
        return jnp.concatenate([tile[:, 0:128], tile[:, 128:256]], axis=0).astype(bf16)

    def col_part(c, state):
        for k in range(8):
            state = col_body(height // 2 + 8 * c + k, state)
        for k in range(4):
            for j in (n // 2 - 4 - 4 * c + k, n // 2 + 4 * c + k):
                vsend[j] = column_tile(j)

                @pl.when(j != me)
                def _():
                    v_copy(j, me).start()

        return state

    lax.fori_loop(0, height // 16, col_part, state)

    vrecv[pl.ds(me, 1)] = vsend[pl.ds(me, 1)]

    row_steps(BEFORE, cols, tuple(state_h[s] for s in range(half)))

    @pl.loop(1, n)
    def _(d):
        other = lax.rem(me + d, n)
        v_copy(other, other).wait()

    skip_h = skip_ref[0:1, :] + skip_ref[1:2, :]

    def finish(p):
        even, other = vrecv[2 * p].astype(f32), vrecv[2 * p + 1].astype(f32)
        even = jnp.concatenate([even[0:8], even[8:16]], axis=1)
        other = jnp.concatenate([other[0:8], other[8:16]], axis=1)
        at = pl.ds(pl.multiple_of(p * 8, 8), 8)
        for r in range(rows):
            if r == 0:
                upright = jnp.where(low4, even, pltpu.roll(other, 4, 0))
            else:
                upright = jnp.where(low4, pltpu.roll(even, 4, 0), other)
            flat = skip_h * cr[r, at, :]
            for source, line in ((ya_h, r), (ya_h, 4 + r), (yb_h, 2 + r), (yb_h, 6 + r)):
                parts = [
                    source[k, pl.ds(p * 64 + line, 8, stride=8), :]
                    for k in range(chans // 128)
                ]
                flat = flat + jnp.concatenate(parts, axis=1)
            combined = flat + upright
            mean = jnp.sum(combined, axis=1, keepdims=True) / chans
            var = jnp.sum(combined * combined, axis=1, keepdims=True) / chans - mean * mean
            scaled = (combined - mean) * lax.rsqrt(var + 1e-05)
            normed[r, at, :] = scaled * gain_ref[...] + nbias_ref[...]

    @pl.loop(0, cols // 32)
    def _(i):
        for k in range(4):
            finish(4 * i + k)

    for r in range(rows):
        out_ref[pl.ds(r, chans, stride=rows), :] = normed[r].T


def fused_device(
    n,
    x_in,
    gate_in,
    conv_weight,
    conv_bias,
    proj_weight,
    dt_weight,
    dt_bias,
    decay_rate,
    skip_gain,
    norm_gain,
    norm_bias,
):
    chans, rows, cols = x_in.shape
    states = decay_rate.shape[2]
    height = rows * n
    f32, bf16 = jnp.float32, jnp.bfloat16
    scratch = [
        pltpu.VMEM((chans * rows, cols), f32),
        pltpu.VMEM((rows, cols, chans), bf16),
        pltpu.VMEM((rows, cols, chans), f32),
        pltpu.VMEM((rows + 2, cols + 16, chans), f32),
        pltpu.VMEM((2, cols, chans), bf16),
        pltpu.VMEM((n, 24, 128), bf16),
        pltpu.VMEM((n, 24, 128), bf16),
        pltpu.VMEM((height + 2, 8, chans), f32),
        pltpu.VMEM((rows, cols, chans), f32),
        pltpu.VMEM((512, chans), f32),
        pltpu.VMEM((2, chans, 256), bf16),
        pltpu.VMEM((512, chans), f32),
        pltpu.VMEM((states // 2, 8, chans), f32),
        pltpu.VMEM((states, 8, chans), f32),
        pltpu.VMEM((cols, 8, chans), f32),
        pltpu.VMEM((cols, 8, chans), f32),
        pltpu.VMEM((cols, 8, 128), f32),
        pltpu.VMEM((chans // 128, cols * 8, 128), f32),
        pltpu.VMEM((chans // 128, cols * 8, 128), f32),
        pltpu.VMEM((states // 2, 8, chans), f32),
        pltpu.VMEM((height, 8, chans), f32),
        pltpu.VMEM((height, 8, chans), f32),
        pltpu.VMEM((height, 8, 128), f32),
        pltpu.VMEM((chans // 128, height * 8, 128), f32),
        pltpu.VMEM((chans // 128, height * 8, 128), f32),
        pltpu.VMEM((n, 16, 128), bf16),
        pltpu.VMEM((n, 16, 128), bf16),
        pltpu.SemaphoreType.DMA((2,)),
        pltpu.SemaphoreType.DMA((2,)),
        pltpu.SemaphoreType.DMA((n,)),
        pltpu.SemaphoreType.DMA((n,)),
        pltpu.SemaphoreType.DMA((n,)),
        pltpu.SemaphoreType.DMA((n,)),
    ]
    operands = (
        x_in.reshape(chans * rows, cols),
        conv_weight.T,
        conv_bias[None, :],
        proj_weight,
        dt_weight.transpose(0, 2, 1),
        dt_bias,
        decay_rate.transpose(0, 2, 1),
        skip_gain,
        norm_gain[None, :],
        norm_bias[None, :],
    )
    held = [pltpu.VMEM(a.shape, a.dtype) for a in operands]
    normed = pl.pallas_call(
        functools.partial(fused_kernel, n),
        out_shape=jax.ShapeDtypeStruct((chans * rows, cols), f32),
        in_specs=[pl.BlockSpec(memory_space=pltpu.HBM)] * len(operands),
        out_specs=pl.BlockSpec(memory_space=pltpu.VMEM),
        scratch_shapes=held + scratch + [pltpu.SemaphoreType.DMA((len(operands),))],
        compiler_params=pltpu.CompilerParams(
            collective_id=0, has_side_effects=True, vmem_limit_bytes=64 * 1024 * 1024
        ),
    )(*operands)
    gate = jax.nn.silu(gate_in.reshape(chans * rows, cols).astype(f32))
    return (normed * gate).astype(bf16).reshape(chans, rows, cols)


def on_device(*args):
    n = lax.axis_size("sp")
    chans, rows, cols = args[0].shape
    rank, states = args[5].shape[2], args[7].shape[2]
    fits = (chans, rows, cols, rank, states) == (256, 2, 4 * n, 8, 16)
    if lax.axis_size("ch") == 1 and fits:
        return fused_device(n, *args)
    return plain_device(*args)


def solution(mesh):
    placed = (
        P("ch", "sp", None),
        P("ch", "sp", None),
        P("ch", None),
        P("ch"),
        P(None, None, "ch"),
        P(None, "ch", None),
        P(None, "ch"),
        P(None, "ch", None),
        P(None, "ch"),
        P("ch"),
        P("ch"),
    )
    return jax.shard_map(
        on_device, mesh=mesh, in_specs=placed, out_specs=P("ch", "sp", None), check_vma=False
    )
```

```python
import functools

import jax
import jax.numpy as jnp
from jax import lax
from jax.experimental import pallas as pl
from jax.experimental.pallas import tpu as pltpu
from jax.sharding import PartitionSpec as P

SPAN = 64
MESH = pl.DeviceIdType.MESH
UNROLL = 16
BEFORE = 64


def with_halo(value, sides, width):
    for axis, dim in sides:
        peers, length = (lax.axis_size(axis), value.shape[dim])
        up = [(i, (i + 1) % peers) for i in range(peers - 1)]
        down = [(j, i) for i, j in up]
        last = lax.slice_in_dim(value, length - width, length, axis=dim)
        first = lax.slice_in_dim(value, 0, width, axis=dim)
        before = lax.ppermute(last, axis, up)
        after = lax.ppermute(first, axis, down)
        value = jnp.concatenate([before, value, after], axis=dim)
    return value


def conv_silu(padded, conv_weight, conv_bias, rows, cols):
    total = jnp.zeros((padded.shape[0], rows, cols), jnp.float32) + conv_bias[:, None, None]
    for offset in range(9):
        down_shift = offset // 3
        side_shift = offset % 3
        window = padded[:, down_shift : down_shift + rows, side_shift : side_shift + cols].astype(
            jnp.float32
        )
        total = total + conv_weight[:, offset][:, None, None] * window
    return jax.nn.silu(total).astype(jnp.bfloat16)


def steps_first(low_rank, dt_weight, dt_bias):
    length, rank, lines = low_rank.shape
    total = jnp.zeros((length, dt_weight.shape[0], lines), jnp.float32) + dt_bias[None, :, None]
    for rank_index in range(rank):
        total = (
            total
            + dt_weight[:, rank_index][None, :, None]
            * low_rank[:, rank_index].astype(jnp.float32)[:, None, :]
        )
    return jax.nn.softplus(total)


def block_scan(values, low_rank, b_coef, c_coef, dt_weight, dt_bias, rates, skip_gain, reverse):
    length, chans, lines = values.shape
    states = rates.shape[1]
    block_len = min(SPAN, length)
    count = length // block_len
    deltas = steps_first(low_rank, dt_weight, dt_bias)
    rates_turned = rates.T[:, :, None]
    skip_column = skip_gain[:, None]

    def single(state, items):
        value_now, delta_now, b_now, c_now = items
        values_now = value_now.astype(jnp.float32)
        decays = jnp.exp(-delta_now[None] * rates_turned)
        state = (
            decays * state + (delta_now * values_now)[None] * b_now.astype(jnp.float32)[:, None, :]
        )
        output = (
            jnp.sum(c_now.astype(jnp.float32)[:, None, :] * state, axis=0)
            + skip_column * values_now
        )
        return (state, output)

    def advance(state, block_items):
        return lax.scan(single, state, block_items, reverse=reverse, unroll=block_len)

    items = (
        values.reshape(count, block_len, chans, lines),
        deltas.reshape(count, block_len, chans, lines),
        b_coef.reshape(count, block_len, states, lines),
        c_coef.reshape(count, block_len, states, lines),
    )
    initial = jnp.zeros((states, chans, lines), jnp.float32)
    _, outputs = lax.scan(advance, initial, items, reverse=reverse)
    return outputs.reshape(length, chans, lines)


def two_directions(values, proj_pair, dt_weight, dt_bias, decay_rate, skip_gain, first):
    rank = dt_weight.shape[2]
    states = decay_rate.shape[2]
    total = jnp.zeros(values.shape, jnp.float32)
    for offset in range(2):
        direction = first + offset
        block = proj_pair[offset]
        total = total + block_scan(
            values,
            block[:, :rank],
            block[:, rank : rank + states],
            block[:, rank + states :],
            dt_weight[direction],
            dt_bias[direction],
            decay_rate[direction],
            skip_gain[direction],
            offset == 1,
        )
    return total


def plain_device(
    x_in,
    gate_in,
    conv_weight,
    conv_bias,
    proj_weight,
    dt_weight,
    dt_bias,
    decay_rate,
    skip_gain,
    norm_gain,
    norm_bias,
):
    chans, rows, cols = x_in.shape
    rank = dt_weight.shape[2]
    states = decay_rate.shape[2]
    width_proj = rank + 2 * states
    padded = with_halo(x_in, (("sp", 1),), 1)
    padded = jnp.pad(padded, ((0, 0), (0, 0), (1, 1)))
    conv_out = conv_silu(padded, conv_weight, conv_bias, rows, cols)
    flattened = conv_out.reshape(chans, rows * cols)
    partial_sum = jnp.dot(
        proj_weight[:2].reshape(2 * width_proj, chans),
        flattened,
        preferred_element_type=jnp.float32,
    )
    row_proj = lax.psum(partial_sum.astype(jnp.bfloat16), "ch").reshape(2, width_proj, rows, cols)
    col_in = lax.all_to_all(conv_out, "sp", split_axis=2, concat_axis=1, tiled=True)
    col_flat = col_in.reshape(chans, col_in.shape[1] * col_in.shape[2])
    col_partial = jnp.dot(
        proj_weight[2:].reshape(2 * width_proj, chans), col_flat, preferred_element_type=jnp.float32
    )
    col_proj = lax.psum(col_partial.astype(jnp.bfloat16), "ch").reshape(
        2, width_proj, col_in.shape[1], col_in.shape[2]
    )
    row_values = conv_out.transpose(2, 0, 1)
    row_pair = row_proj.transpose(0, 3, 1, 2)
    horizontal = two_directions(
        row_values, row_pair, dt_weight, dt_bias, decay_rate, skip_gain, 0
    ).transpose(1, 2, 0)
    col_values = col_in.transpose(1, 0, 2)
    col_pair = col_proj.transpose(0, 2, 1, 3)
    vertical = two_directions(col_values, col_pair, dt_weight, dt_bias, decay_rate, skip_gain, 2)
    vertical = vertical.transpose(1, 0, 2).astype(jnp.bfloat16)
    vertical_rows = lax.all_to_all(vertical, "sp", split_axis=1, concat_axis=2, tiled=True)
    combined = horizontal + vertical_rows.astype(jnp.float32)
    sum_first, sum_second = lax.psum(
        (jnp.sum(combined, axis=0), jnp.sum(combined * combined, axis=0)), "ch"
    )
    chans_total = chans * lax.axis_size("ch")
    mean = sum_first / chans_total
    var = sum_second / chans_total - mean * mean
    normed = (combined - mean[None]) * lax.rsqrt(var[None] + 1e-05) * norm_gain[
        :, None, None
    ] + norm_bias[:, None, None]
    return (normed * jax.nn.silu(gate_in.astype(jnp.float32))).astype(jnp.bfloat16)


def fused_kernel(n, *refs):
    sources, out_ref, held = refs[:11], refs[11], refs[12:23]
    (
        x_ref,
        cw_ref,
        cb_ref,
        pw_ref,
        dw_ref,
        db_ref,
        rate_ref,
        skip_ref,
        gain_ref,
        nbias_ref,
        gate_ref,
    ) = held
    (
        xs,
        xt,
        normed,
        xpad,
        halo,
        xsend,
        xrecv,
        xv,
        cr,
        wf,
        wt,
        wd,
        rate_h,
        rate_v,
        u_h,
        d_h,
        p_h,
        ya_h,
        yb_h,
        state_h,
        u_v,
        d_v,
        p_v,
        ya_v,
        yb_v,
        vsend,
        vrecv,
        halo_send,
        halo_recv,
        xs_sem,
        xr_sem,
        vs_sem,
        vr_sem,
        in_sem,
    ) = refs[23:]
    rows, cols, chans = cr.shape
    height = rows * n
    rank = dw_ref.shape[1]
    states = rate_ref.shape[1]
    width = rank + 2 * states
    half = states // 2
    f32, bf16 = jnp.float32, jnp.bfloat16
    me = lax.axis_index("sp")
    right, left = lax.rem(me + 1, n), lax.rem(me + n - 1, n)

    loads = [
        pltpu.make_async_copy(source, target, in_sem.at[i])
        for i, (source, target) in enumerate(zip(sources, held))
    ]
    for load in loads:
        load.start()

    barrier = pltpu.get_barrier_semaphore()

    @pl.loop(1, n)
    def _(d):
        pl.semaphore_signal(
            barrier, inc=1, device_id={"sp": lax.rem(me + d, n)}, device_id_type=MESH
        )

    low4_one = lax.broadcasted_iota(jnp.int32, (8, 128), 0) < 4
    low6 = lax.broadcasted_iota(jnp.int32, (8, chans), 0) < 6

    edge = jnp.zeros((rows + 2, 8, chans), f32)
    xpad[:, 0:8, :] = edge
    xpad[:, cols + 8 : cols + 16, :] = edge
    loads[0].wait()
    xs[...] = x_ref[...].astype(f32)
    for r in range(rows):
        upright = xs[pl.ds(r, chans, stride=rows), :].T
        xpad[r + 1, 8 : cols + 8, :] = upright
        xt[r] = upright.astype(bf16)
    for j in range(n):
        at = 8 + 4 * j - 1
        first, second = xpad[1, at : at + 8, :], xpad[2, at : at + 8, :]
        lower = jnp.where(low6, first, pltpu.roll(second, 6, 0))
        rest = pltpu.roll(second, 6, 0)
        near, far = rest[:, 0:128], pltpu.roll(rest[:, 128:256], 4, 0)
        xsend[j] = jnp.concatenate(
            [lower[:, 0:128], lower[:, 128:256], jnp.where(low4_one, near, far)], axis=0
        ).astype(bf16)
    xrecv[pl.ds(me, 1)] = xsend[pl.ds(me, 1)]

    pl.semaphore_wait(barrier, n - 1)

    def halo_copy(which):
        return pltpu.make_async_remote_copy(
            src_ref=xt.at[rows - 1 if which == 0 else 0],
            dst_ref=halo.at[which],
            send_sem=halo_send.at[which],
            recv_sem=halo_recv.at[which],
            device_id={"sp": right if which == 0 else left},
            device_id_type=MESH,
        )

    halo_copy(0).start()
    halo_copy(1).start()

    def x_copy(d, slot):
        dst = lax.rem(me + d, n)
        return pltpu.make_async_remote_copy(
            src_ref=xsend.at[dst],
            dst_ref=xrecv.at[slot],
            send_sem=xs_sem.at[d],
            recv_sem=xr_sem.at[d],
            device_id={"sp": dst},
            device_id_type=MESH,
        )

    def v_copy(dst, slot):
        return pltpu.make_async_remote_copy(
            src_ref=vsend.at[dst],
            dst_ref=vrecv.at[slot],
            send_sem=vs_sem.at[dst],
            recv_sem=vr_sem.at[slot],
            device_id={"sp": dst},
            device_id_type=MESH,
        )

    @pl.loop(1, n)
    def _(d):
        x_copy(d, me).start()

    sub = lax.broadcasted_iota(jnp.int32, (8, chans), 0)
    low4 = sub < 4
    low2 = sub < 2
    dir_h = (sub // 2) % 2 == 0
    dir_v = low4
    for load in loads[1:]:
        load.wait()
    wf[...] = jnp.zeros(wf.shape, f32)
    wd[...] = jnp.zeros(wd.shape, f32)
    for k in range(4):
        base = 128 * k
        rowsw = pw_ref[k].astype(f32)
        wf[base : base + width, :] = rowsw
        wf[base + width : base + width + rank, :] = rowsw[0:rank]
        full = dw_ref[k]
        high = full.astype(bf16).astype(f32)
        wd[base : base + rank, :] = high
        wd[base + width : base + width + rank, :] = full - high
    for first in range(2):
        wt[first] = wf[256 * first : 256 * first + 256, :].T.astype(bf16)
    for s in range(states):
        rate_v[s] = -jnp.where(
            dir_v, rate_ref[2, s : s + 1, :], rate_ref[3, s : s + 1, :]
        )
    for s in range(half):
        lower = jnp.where(dir_h, rate_ref[0, s : s + 1, :], rate_ref[1, s : s + 1, :])
        upper = jnp.where(
            dir_h, rate_ref[0, s + half : s + half + 1, :], rate_ref[1, s + half : s + half + 1, :]
        )
        rate_h[s] = -jnp.where(low4, lower, upper)

    def prepare(steps, first, dirs, u, dl, p, halves):
        weights = wt[first]
        up = wd[256 * first : 256 * first + 256, :].astype(bf16)
        bias = jnp.where(dirs, db_ref[2 * first : 2 * first + 1], db_ref[2 * first + 1 : 2 * first + 2])
        bias = bias[None]
        pick = dirs[:, 0:128][None]
        lift = low4_one[None]
        size = 32

        @pl.loop(0, steps // size)
        def _(i):
            at = pl.ds(i * size, size)
            flat = u[at].reshape(size * 8, chans).astype(bf16)
            proj = lax.dot_general(
                flat, weights, (((1,), (0,)), ((), ())), preferred_element_type=f32
            )
            proj = proj.astype(bf16).astype(f32).reshape(size, 8, 256)
            one, two = proj[:, :, 0:128], proj[:, :, 128:256]
            own = jnp.where(pick, one, two)
            both = jnp.concatenate(
                [jnp.where(pick, one, 0.0), jnp.where(pick, 0.0, two)], axis=2
            )
            pre = jnp.dot(
                both.reshape(size * 8, 256).astype(bf16), up, preferred_element_type=f32
            ).reshape(size, 8, chans)
            pre = pre + bias
            dl[at] = jnp.maximum(pre, 0.0) + jnp.log(1.0 + jnp.exp(-jnp.abs(pre)))
            if halves:
                own = jnp.where(lift, own, pltpu.roll(own, 128 - half, 2))
            p[at] = own

    def across(column):
        return jnp.concatenate([jnp.broadcast_to(column, (8, 128))] * (chans // 128), axis=1)

    def step(t, state, u, dl, p, rate, ya, yb, last, count, offset):
        delta, tile = dl[t], p[t]
        drive = delta * u[t]
        total = None
        new = []
        for s in range(count):
            decay = jnp.exp(delta * rate[s])
            b_now = across(tile[:, rank + s : rank + s + 1])
            c_now = across(tile[:, offset + s : offset + s + 1])
            now = decay * state[s] + drive * b_now
            new.append(now)
            term = c_now * now
            total = term if total is None else total + term
        for k in range(chans // 128):
            piece = total[:, k * 128 : k * 128 + 128]
            ya[k, pl.ds(pl.multiple_of(t * 8, 8), 8), :] = piece
            yb[k, pl.ds(pl.multiple_of((last - t) * 8, 8), 8), :] = piece
        return tuple(new)

    for which in range(2):
        halo_copy(which).wait()
    above, below = halo[0].astype(f32), halo[1].astype(f32)
    xpad[0, 8 : cols + 8, :] = jnp.where(me == 0, jnp.zeros_like(above), above)
    xpad[rows + 1, 8 : cols + 8, :] = jnp.where(me == n - 1, jnp.zeros_like(below), below)
    block = 32
    for r in range(rows):
        for c in range(0, cols, block):
            total = jnp.zeros((block, chans), f32) + cb_ref[...]
            for i in range(3):
                for j in range(3):
                    window = xpad[r + i, 7 + c + j : 7 + c + j + block, :]
                    total = total + cw_ref[3 * i + j : 3 * i + j + 1, :] * window
            cr[r, c : c + block, :] = jax.nn.silu(total).astype(bf16).astype(f32)

    odd = sub % 2 == 1

    def spread(t):
        ahead = jnp.where(odd, cr[1, pl.ds(t, 1), :], cr[0, pl.ds(t, 1), :])
        back = jnp.where(odd, cr[1, pl.ds(cols - 1 - t, 1), :], cr[0, pl.ds(cols - 1 - t, 1), :])
        u_h[t] = jnp.where(dir_h, ahead, back)

    @pl.loop(0, cols // 8)
    def _(i):
        for k in range(8):
            spread(i * 8 + k)

    prepare(cols, 0, dir_h, u_h, d_h, p_h, True)

    def row_steps(lower, upper, state):
        def body(t, state):
            return step(
                t, state, u_h, d_h, p_h, rate_h, ya_h, yb_h, cols - 1, half, rank + states
            )

        return lax.fori_loop(lower, upper, body, state, unroll=UNROLL)

    state = row_steps(0, BEFORE, tuple(jnp.zeros((8, chans), f32) for _ in range(half)))
    for s in range(half):
        state_h[s] = state[s]

    @pl.loop(1, n)
    def _(d):
        x_copy(d, lax.rem(me + n - d, n)).wait()

    nothing = jnp.zeros((8, chans), f32)
    xv[0] = nothing
    xv[height + 1] = nothing

    @pl.loop(0, n)
    def _(j):
        tiles = xrecv[j].astype(f32)
        rest = tiles[16:24]
        lower = jnp.concatenate([tiles[0:8], tiles[8:16]], axis=1)
        rest = jnp.concatenate([rest, pltpu.roll(rest, 4, 0)], axis=1)
        xv[1 + 2 * j] = lower
        xv[2 + 2 * j] = jnp.where(low2, pltpu.roll(lower, 2, 0), pltpu.roll(rest, 2, 0))

    def conv_step(t):
        total = jnp.zeros((8, chans), f32) + cb_ref[...]
        tiles = [xv[t], xv[t + 1], xv[t + 2]]
        for j in range(3):
            part = None
            for i in range(3):
                term = cw_ref[3 * i + j : 3 * i + j + 1, :] * tiles[i]
                part = term if part is None else part + term
            total = total + pltpu.roll(part, (8 - j) % 8, 0)
        value = jax.nn.silu(total).astype(bf16).astype(f32)
        turned = pltpu.roll(value, 4, 0)
        u_v[t, 0:4, :] = value[0:4]
        u_v[height - 1 - t, 4:8, :] = turned[4:8]

    @pl.loop(0, height // 8)
    def _(i):
        for k in range(8):
            conv_step(i * 8 + k)

    prepare(height, 1, dir_v, u_v, d_v, p_v, False)

    def col_body(t, state):
        return step(
            t, state, u_v, d_v, p_v, rate_v, ya_v, yb_v, height - 1, states, rank + states
        )

    state = lax.fori_loop(
        0, height // 2, col_body, tuple(jnp.zeros((8, chans), f32) for _ in range(states)), unroll=UNROLL
    )

    skip_v = skip_ref[2:3, :] + skip_ref[3:4, :]

    def column_row(t):
        at = pl.ds(pl.multiple_of(t * 8, 8), 8)
        parts = [
            ya_v[k, at, :] + pltpu.roll(yb_v[k, at, :], 4, 0) for k in range(chans // 128)
        ]
        return jnp.concatenate(parts, axis=1) + skip_v * u_v[t]

    def column_tile(j):
        tile = jnp.where(low4, column_row(2 * j), pltpu.roll(column_row(2 * j + 1), 4, 0))
        return jnp.concatenate([tile[:, 0:128], tile[:, 128:256]], axis=0).astype(bf16)

    def col_part(c, state):
        for k in range(8):
            state = col_body(height // 2 + 8 * c + k, state)
        for k in range(4):
            for j in (n // 2 - 4 - 4 * c + k, n // 2 + 4 * c + k):
                vsend[j] = column_tile(j)

                @pl.when(j != me)
                def _():
                    v_copy(j, me).start()

        return state

    lax.fori_loop(0, height // 16, col_part, state)

    vrecv[pl.ds(me, 1)] = vsend[pl.ds(me, 1)]

    row_steps(BEFORE, cols, tuple(state_h[s] for s in range(half)))

    @pl.loop(1, n)
    def _(d):
        other = lax.rem(me + d, n)
        v_copy(other, other).wait()

    skip_h = skip_ref[0:1, :] + skip_ref[1:2, :]

    def finish(p):
        even, other = vrecv[2 * p].astype(f32), vrecv[2 * p + 1].astype(f32)
        even = jnp.concatenate([even[0:8], even[8:16]], axis=1)
        other = jnp.concatenate([other[0:8], other[8:16]], axis=1)
        at = pl.ds(pl.multiple_of(p * 8, 8), 8)
        for r in range(rows):
            if r == 0:
                upright = jnp.where(low4, even, pltpu.roll(other, 4, 0))
            else:
                upright = jnp.where(low4, pltpu.roll(even, 4, 0), other)
            flat = skip_h * cr[r, at, :]
            for source, line in ((ya_h, r), (ya_h, 4 + r), (yb_h, 2 + r), (yb_h, 6 + r)):
                parts = [
                    source[k, pl.ds(p * 64 + line, 8, stride=8), :]
                    for k in range(chans // 128)
                ]
                flat = flat + jnp.concatenate(parts, axis=1)
            combined = flat + upright
            mean = jnp.sum(combined, axis=1, keepdims=True) / chans
            var = jnp.sum(combined * combined, axis=1, keepdims=True) / chans - mean * mean
            scaled = (combined - mean) * lax.rsqrt(var + 1e-05)
            normed[r, at, :] = scaled * gain_ref[...] + nbias_ref[...]

    @pl.loop(0, cols // 32)
    def _(i):
        for k in range(4):
            finish(4 * i + k)

    for r in range(rows):
        xs[pl.ds(r, chans, stride=rows), :] = normed[r].T
    out_ref[...] = (xs[...] * jax.nn.silu(gate_ref[...].astype(f32))).astype(bf16)


def fused_device(
    n,
    x_in,
    gate_in,
    conv_weight,
    conv_bias,
    proj_weight,
    dt_weight,
    dt_bias,
    decay_rate,
    skip_gain,
    norm_gain,
    norm_bias,
):
    chans, rows, cols = x_in.shape
    states = decay_rate.shape[2]
    height = rows * n
    f32, bf16 = jnp.float32, jnp.bfloat16
    scratch = [
        pltpu.VMEM((chans * rows, cols), f32),
        pltpu.VMEM((rows, cols, chans), bf16),
        pltpu.VMEM((rows, cols, chans), f32),
        pltpu.VMEM((rows + 2, cols + 16, chans), f32),
        pltpu.VMEM((2, cols, chans), bf16),
        pltpu.VMEM((n, 24, 128), bf16),
        pltpu.VMEM((n, 24, 128), bf16),
        pltpu.VMEM((height + 2, 8, chans), f32),
        pltpu.VMEM((rows, cols, chans), f32),
        pltpu.VMEM((512, chans), f32),
        pltpu.VMEM((2, chans, 256), bf16),
        pltpu.VMEM((512, chans), f32),
        pltpu.VMEM((states // 2, 8, chans), f32),
        pltpu.VMEM((states, 8, chans), f32),
        pltpu.VMEM((cols, 8, chans), f32),
        pltpu.VMEM((cols, 8, chans), f32),
        pltpu.VMEM((cols, 8, 128), f32),
        pltpu.VMEM((chans // 128, cols * 8, 128), f32),
        pltpu.VMEM((chans // 128, cols * 8, 128), f32),
        pltpu.VMEM((states // 2, 8, chans), f32),
        pltpu.VMEM((height, 8, chans), f32),
        pltpu.VMEM((height, 8, chans), f32),
        pltpu.VMEM((height, 8, 128), f32),
        pltpu.VMEM((chans // 128, height * 8, 128), f32),
        pltpu.VMEM((chans // 128, height * 8, 128), f32),
        pltpu.VMEM((n, 16, 128), bf16),
        pltpu.VMEM((n, 16, 128), bf16),
        pltpu.SemaphoreType.DMA((2,)),
        pltpu.SemaphoreType.DMA((2,)),
        pltpu.SemaphoreType.DMA((n,)),
        pltpu.SemaphoreType.DMA((n,)),
        pltpu.SemaphoreType.DMA((n,)),
        pltpu.SemaphoreType.DMA((n,)),
    ]
    operands = (
        x_in.reshape(chans * rows, cols),
        conv_weight.T,
        conv_bias[None, :],
        proj_weight,
        dt_weight.transpose(0, 2, 1),
        dt_bias,
        decay_rate.transpose(0, 2, 1),
        skip_gain,
        norm_gain[None, :],
        norm_bias[None, :],
        gate_in.reshape(chans * rows, cols),
    )
    held = [pltpu.VMEM(a.shape, a.dtype) for a in operands]
    mixed = pl.pallas_call(
        functools.partial(fused_kernel, n),
        out_shape=jax.ShapeDtypeStruct((chans * rows, cols), bf16),
        in_specs=[pl.BlockSpec(memory_space=pltpu.HBM)] * len(operands),
        out_specs=pl.BlockSpec(memory_space=pltpu.VMEM),
        scratch_shapes=held + scratch + [pltpu.SemaphoreType.DMA((len(operands),))],
        compiler_params=pltpu.CompilerParams(
            collective_id=0, has_side_effects=True, vmem_limit_bytes=64 * 1024 * 1024
        ),
    )(*operands)
    return mixed.reshape(chans, rows, cols)


def on_device(*args):
    n = lax.axis_size("sp")
    chans, rows, cols = args[0].shape
    rank, states = args[5].shape[2], args[7].shape[2]
    fits = (chans, rows, cols, rank, states) == (256, 2, 4 * n, 8, 16)
    if lax.axis_size("ch") == 1 and fits:
        return fused_device(n, *args)
    return plain_device(*args)


def solution(mesh):
    placed = (
        P("ch", "sp", None),
        P("ch", "sp", None),
        P("ch", None),
        P("ch"),
        P(None, None, "ch"),
        P(None, "ch", None),
        P(None, "ch"),
        P(None, "ch", None),
        P(None, "ch"),
        P("ch"),
        P("ch"),
    )
    return jax.shard_map(
        on_device, mesh=mesh, in_specs=placed, out_specs=P("ch", "sp", None), check_vma=False
    )
```

```python
import functools

import jax
import jax.numpy as jnp
from jax import lax
from jax.experimental import pallas as pl
from jax.experimental.pallas import tpu as pltpu
from jax.sharding import PartitionSpec as P

SPAN = 64
MESH = pl.DeviceIdType.MESH
UNROLL = 16
BEFORE = 96


def with_halo(value, sides, width):
    for axis, dim in sides:
        peers, length = (lax.axis_size(axis), value.shape[dim])
        up = [(i, (i + 1) % peers) for i in range(peers - 1)]
        down = [(j, i) for i, j in up]
        last = lax.slice_in_dim(value, length - width, length, axis=dim)
        first = lax.slice_in_dim(value, 0, width, axis=dim)
        before = lax.ppermute(last, axis, up)
        after = lax.ppermute(first, axis, down)
        value = jnp.concatenate([before, value, after], axis=dim)
    return value


def conv_silu(padded, conv_weight, conv_bias, rows, cols):
    total = jnp.zeros((padded.shape[0], rows, cols), jnp.float32) + conv_bias[:, None, None]
    for offset in range(9):
        down_shift = offset // 3
        side_shift = offset % 3
        window = padded[:, down_shift : down_shift + rows, side_shift : side_shift + cols].astype(
            jnp.float32
        )
        total = total + conv_weight[:, offset][:, None, None] * window
    return jax.nn.silu(total).astype(jnp.bfloat16)


def steps_first(low_rank, dt_weight, dt_bias):
    length, rank, lines = low_rank.shape
    total = jnp.zeros((length, dt_weight.shape[0], lines), jnp.float32) + dt_bias[None, :, None]
    for rank_index in range(rank):
        total = (
            total
            + dt_weight[:, rank_index][None, :, None]
            * low_rank[:, rank_index].astype(jnp.float32)[:, None, :]
        )
    return jax.nn.softplus(total)


def block_scan(values, low_rank, b_coef, c_coef, dt_weight, dt_bias, rates, skip_gain, reverse):
    length, chans, lines = values.shape
    states = rates.shape[1]
    block_len = min(SPAN, length)
    count = length // block_len
    deltas = steps_first(low_rank, dt_weight, dt_bias)
    rates_turned = rates.T[:, :, None]
    skip_column = skip_gain[:, None]

    def single(state, items):
        value_now, delta_now, b_now, c_now = items
        values_now = value_now.astype(jnp.float32)
        decays = jnp.exp(-delta_now[None] * rates_turned)
        state = (
            decays * state + (delta_now * values_now)[None] * b_now.astype(jnp.float32)[:, None, :]
        )
        output = (
            jnp.sum(c_now.astype(jnp.float32)[:, None, :] * state, axis=0)
            + skip_column * values_now
        )
        return (state, output)

    def advance(state, block_items):
        return lax.scan(single, state, block_items, reverse=reverse, unroll=block_len)

    items = (
        values.reshape(count, block_len, chans, lines),
        deltas.reshape(count, block_len, chans, lines),
        b_coef.reshape(count, block_len, states, lines),
        c_coef.reshape(count, block_len, states, lines),
    )
    initial = jnp.zeros((states, chans, lines), jnp.float32)
    _, outputs = lax.scan(advance, initial, items, reverse=reverse)
    return outputs.reshape(length, chans, lines)


def two_directions(values, proj_pair, dt_weight, dt_bias, decay_rate, skip_gain, first):
    rank = dt_weight.shape[2]
    states = decay_rate.shape[2]
    total = jnp.zeros(values.shape, jnp.float32)
    for offset in range(2):
        direction = first + offset
        block = proj_pair[offset]
        total = total + block_scan(
            values,
            block[:, :rank],
            block[:, rank : rank + states],
            block[:, rank + states :],
            dt_weight[direction],
            dt_bias[direction],
            decay_rate[direction],
            skip_gain[direction],
            offset == 1,
        )
    return total


def plain_device(
    x_in,
    gate_in,
    conv_weight,
    conv_bias,
    proj_weight,
    dt_weight,
    dt_bias,
    decay_rate,
    skip_gain,
    norm_gain,
    norm_bias,
):
    chans, rows, cols = x_in.shape
    rank = dt_weight.shape[2]
    states = decay_rate.shape[2]
    width_proj = rank + 2 * states
    padded = with_halo(x_in, (("sp", 1),), 1)
    padded = jnp.pad(padded, ((0, 0), (0, 0), (1, 1)))
    conv_out = conv_silu(padded, conv_weight, conv_bias, rows, cols)
    flattened = conv_out.reshape(chans, rows * cols)
    partial_sum = jnp.dot(
        proj_weight[:2].reshape(2 * width_proj, chans),
        flattened,
        preferred_element_type=jnp.float32,
    )
    row_proj = lax.psum(partial_sum.astype(jnp.bfloat16), "ch").reshape(2, width_proj, rows, cols)
    col_in = lax.all_to_all(conv_out, "sp", split_axis=2, concat_axis=1, tiled=True)
    col_flat = col_in.reshape(chans, col_in.shape[1] * col_in.shape[2])
    col_partial = jnp.dot(
        proj_weight[2:].reshape(2 * width_proj, chans), col_flat, preferred_element_type=jnp.float32
    )
    col_proj = lax.psum(col_partial.astype(jnp.bfloat16), "ch").reshape(
        2, width_proj, col_in.shape[1], col_in.shape[2]
    )
    row_values = conv_out.transpose(2, 0, 1)
    row_pair = row_proj.transpose(0, 3, 1, 2)
    horizontal = two_directions(
        row_values, row_pair, dt_weight, dt_bias, decay_rate, skip_gain, 0
    ).transpose(1, 2, 0)
    col_values = col_in.transpose(1, 0, 2)
    col_pair = col_proj.transpose(0, 2, 1, 3)
    vertical = two_directions(col_values, col_pair, dt_weight, dt_bias, decay_rate, skip_gain, 2)
    vertical = vertical.transpose(1, 0, 2).astype(jnp.bfloat16)
    vertical_rows = lax.all_to_all(vertical, "sp", split_axis=1, concat_axis=2, tiled=True)
    combined = horizontal + vertical_rows.astype(jnp.float32)
    sum_first, sum_second = lax.psum(
        (jnp.sum(combined, axis=0), jnp.sum(combined * combined, axis=0)), "ch"
    )
    chans_total = chans * lax.axis_size("ch")
    mean = sum_first / chans_total
    var = sum_second / chans_total - mean * mean
    normed = (combined - mean[None]) * lax.rsqrt(var[None] + 1e-05) * norm_gain[
        :, None, None
    ] + norm_bias[:, None, None]
    return (normed * jax.nn.silu(gate_in.astype(jnp.float32))).astype(jnp.bfloat16)


def fused_kernel(n, *refs):
    sources, out_ref, held = refs[:11], refs[11], refs[12:23]
    (
        x_ref,
        cw_ref,
        cb_ref,
        pw_ref,
        dw_ref,
        db_ref,
        rate_ref,
        skip_ref,
        gain_ref,
        nbias_ref,
        gate_ref,
    ) = held
    (
        xs,
        xt,
        normed,
        xpad,
        halo,
        xsend,
        xrecv,
        xv,
        cr,
        wf,
        wt,
        wd,
        rate_h,
        rate_v,
        u_h,
        d_h,
        p_h,
        ya_h,
        yb_h,
        state_h,
        u_v,
        d_v,
        p_v,
        ya_v,
        yb_v,
        vsend,
        vrecv,
        halo_send,
        halo_recv,
        xs_sem,
        xr_sem,
        vs_sem,
        vr_sem,
        in_sem,
    ) = refs[23:]
    rows, cols, chans = cr.shape
    height = rows * n
    rank = dw_ref.shape[1]
    states = rate_ref.shape[1]
    width = rank + 2 * states
    half = states // 2
    f32, bf16 = jnp.float32, jnp.bfloat16
    me = lax.axis_index("sp")
    right, left = lax.rem(me + 1, n), lax.rem(me + n - 1, n)

    loads = [
        pltpu.make_async_copy(source, target, in_sem.at[i])
        for i, (source, target) in enumerate(zip(sources, held))
    ]
    for load in loads:
        load.start()

    barrier = pltpu.get_barrier_semaphore()

    @pl.loop(1, n)
    def _(d):
        pl.semaphore_signal(
            barrier, inc=1, device_id={"sp": lax.rem(me + d, n)}, device_id_type=MESH
        )

    low4_one = lax.broadcasted_iota(jnp.int32, (8, 128), 0) < 4
    low6 = lax.broadcasted_iota(jnp.int32, (8, chans), 0) < 6

    edge = jnp.zeros((rows + 2, 8, chans), f32)
    xpad[:, 0:8, :] = edge
    xpad[:, cols + 8 : cols + 16, :] = edge
    loads[0].wait()
    xs[...] = x_ref[...].astype(f32)
    for r in range(rows):
        upright = xs[pl.ds(r, chans, stride=rows), :].T
        xpad[r + 1, 8 : cols + 8, :] = upright
        xt[r] = upright.astype(bf16)
    for j in range(n):
        at = 8 + 4 * j - 1
        first, second = xpad[1, at : at + 8, :], xpad[2, at : at + 8, :]
        lower = jnp.where(low6, first, pltpu.roll(second, 6, 0))
        rest = pltpu.roll(second, 6, 0)
        near, far = rest[:, 0:128], pltpu.roll(rest[:, 128:256], 4, 0)
        xsend[j] = jnp.concatenate(
            [lower[:, 0:128], lower[:, 128:256], jnp.where(low4_one, near, far)], axis=0
        ).astype(bf16)
    xrecv[pl.ds(me, 1)] = xsend[pl.ds(me, 1)]

    pl.semaphore_wait(barrier, n - 1)

    def halo_copy(which):
        return pltpu.make_async_remote_copy(
            src_ref=xt.at[rows - 1 if which == 0 else 0],
            dst_ref=halo.at[which],
            send_sem=halo_send.at[which],
            recv_sem=halo_recv.at[which],
            device_id={"sp": right if which == 0 else left},
            device_id_type=MESH,
        )

    halo_copy(0).start()
    halo_copy(1).start()

    def x_copy(d, slot):
        dst = lax.rem(me + d, n)
        return pltpu.make_async_remote_copy(
            src_ref=xsend.at[dst],
            dst_ref=xrecv.at[slot],
            send_sem=xs_sem.at[d],
            recv_sem=xr_sem.at[d],
            device_id={"sp": dst},
            device_id_type=MESH,
        )

    def v_copy(dst, slot):
        return pltpu.make_async_remote_copy(
            src_ref=vsend.at[dst],
            dst_ref=vrecv.at[slot],
            send_sem=vs_sem.at[dst],
            recv_sem=vr_sem.at[slot],
            device_id={"sp": dst},
            device_id_type=MESH,
        )

    @pl.loop(1, n)
    def _(d):
        x_copy(d, me).start()

    sub = lax.broadcasted_iota(jnp.int32, (8, chans), 0)
    low4 = sub < 4
    low2 = sub < 2
    dir_h = (sub // 2) % 2 == 0
    dir_v = low4
    for load in loads[1:]:
        load.wait()
    wf[...] = jnp.zeros(wf.shape, f32)
    wd[...] = jnp.zeros(wd.shape, f32)
    for k in range(4):
        base = 128 * k
        rowsw = pw_ref[k].astype(f32)
        wf[base : base + width, :] = rowsw
        wf[base + width : base + width + rank, :] = rowsw[0:rank]
        full = dw_ref[k]
        high = full.astype(bf16).astype(f32)
        wd[base : base + rank, :] = high
        wd[base + width : base + width + rank, :] = full - high
    for first in range(2):
        wt[first] = wf[256 * first : 256 * first + 256, :].T.astype(bf16)
    for s in range(states):
        rate_v[s] = -jnp.where(
            dir_v, rate_ref[2, s : s + 1, :], rate_ref[3, s : s + 1, :]
        )
    for s in range(half):
        lower = jnp.where(dir_h, rate_ref[0, s : s + 1, :], rate_ref[1, s : s + 1, :])
        upper = jnp.where(
            dir_h, rate_ref[0, s + half : s + half + 1, :], rate_ref[1, s + half : s + half + 1, :]
        )
        rate_h[s] = -jnp.where(low4, lower, upper)

    def prepare(steps, first, dirs, u, dl, p, halves):
        weights = wt[first]
        up = wd[256 * first : 256 * first + 256, :].astype(bf16)
        bias = jnp.where(dirs, db_ref[2 * first : 2 * first + 1], db_ref[2 * first + 1 : 2 * first + 2])
        bias = bias[None]
        pick = dirs[:, 0:128][None]
        lift = low4_one[None]
        size = 32

        @pl.loop(0, steps // size)
        def _(i):
            at = pl.ds(i * size, size)
            flat = u[at].reshape(size * 8, chans).astype(bf16)
            proj = lax.dot_general(
                flat, weights, (((1,), (0,)), ((), ())), preferred_element_type=f32
            )
            proj = proj.astype(bf16).astype(f32).reshape(size, 8, 256)
            one, two = proj[:, :, 0:128], proj[:, :, 128:256]
            own = jnp.where(pick, one, two)
            both = jnp.concatenate(
                [jnp.where(pick, one, 0.0), jnp.where(pick, 0.0, two)], axis=2
            )
            pre = jnp.dot(
                both.reshape(size * 8, 256).astype(bf16), up, preferred_element_type=f32
            ).reshape(size, 8, chans)
            pre = pre + bias
            dl[at] = jnp.maximum(pre, 0.0) + jnp.log(1.0 + jnp.exp(-jnp.abs(pre)))
            if halves:
                own = jnp.where(lift, own, pltpu.roll(own, 128 - half, 2))
            p[at] = own

    def across(column):
        return jnp.concatenate([jnp.broadcast_to(column, (8, 128))] * (chans // 128), axis=1)

    def step(t, state, u, dl, p, rate, ya, yb, last, count, offset):
        delta, tile = dl[t], p[t]
        drive = delta * u[t]
        total = None
        new = []
        for s in range(count):
            decay = jnp.exp(delta * rate[s])
            b_now = across(tile[:, rank + s : rank + s + 1])
            c_now = across(tile[:, offset + s : offset + s + 1])
            now = decay * state[s] + drive * b_now
            new.append(now)
            term = c_now * now
            total = term if total is None else total + term
        for k in range(chans // 128):
            piece = total[:, k * 128 : k * 128 + 128]
            ya[k, pl.ds(pl.multiple_of(t * 8, 8), 8), :] = piece
            yb[k, pl.ds(pl.multiple_of((last - t) * 8, 8), 8), :] = piece
        return tuple(new)

    for which in range(2):
        halo_copy(which).wait()
    above, below = halo[0].astype(f32), halo[1].astype(f32)
    xpad[0, 8 : cols + 8, :] = jnp.where(me == 0, jnp.zeros_like(above), above)
    xpad[rows + 1, 8 : cols + 8, :] = jnp.where(me == n - 1, jnp.zeros_like(below), below)
    block = 32
    for r in range(rows):
        for c in range(0, cols, block):
            total = jnp.zeros((block, chans), f32) + cb_ref[...]
            for i in range(3):
                for j in range(3):
                    window = xpad[r + i, 7 + c + j : 7 + c + j + block, :]
                    total = total + cw_ref[3 * i + j : 3 * i + j + 1, :] * window
            cr[r, c : c + block, :] = jax.nn.silu(total).astype(bf16).astype(f32)

    odd = sub % 2 == 1

    def spread(t):
        ahead = jnp.where(odd, cr[1, pl.ds(t, 1), :], cr[0, pl.ds(t, 1), :])
        back = jnp.where(odd, cr[1, pl.ds(cols - 1 - t, 1), :], cr[0, pl.ds(cols - 1 - t, 1), :])
        u_h[t] = jnp.where(dir_h, ahead, back)

    @pl.loop(0, cols // 8)
    def _(i):
        for k in range(8):
            spread(i * 8 + k)

    prepare(cols, 0, dir_h, u_h, d_h, p_h, True)

    def row_steps(lower, upper, state):
        def body(t, state):
            return step(
                t, state, u_h, d_h, p_h, rate_h, ya_h, yb_h, cols - 1, half, rank + states
            )

        return lax.fori_loop(lower, upper, body, state, unroll=UNROLL)

    state = row_steps(0, BEFORE, tuple(jnp.zeros((8, chans), f32) for _ in range(half)))
    for s in range(half):
        state_h[s] = state[s]

    @pl.loop(1, n)
    def _(d):
        x_copy(d, lax.rem(me + n - d, n)).wait()

    nothing = jnp.zeros((8, chans), f32)
    xv[0] = nothing
    xv[height + 1] = nothing

    @pl.loop(0, n)
    def _(j):
        tiles = xrecv[j].astype(f32)
        rest = tiles[16:24]
        lower = jnp.concatenate([tiles[0:8], tiles[8:16]], axis=1)
        rest = jnp.concatenate([rest, pltpu.roll(rest, 4, 0)], axis=1)
        xv[1 + 2 * j] = lower
        xv[2 + 2 * j] = jnp.where(low2, pltpu.roll(lower, 2, 0), pltpu.roll(rest, 2, 0))

    def conv_step(t):
        total = jnp.zeros((8, chans), f32) + cb_ref[...]
        tiles = [xv[t], xv[t + 1], xv[t + 2]]
        for j in range(3):
            part = None
            for i in range(3):
                term = cw_ref[3 * i + j : 3 * i + j + 1, :] * tiles[i]
                part = term if part is None else part + term
            total = total + pltpu.roll(part, (8 - j) % 8, 0)
        value = jax.nn.silu(total).astype(bf16).astype(f32)
        turned = pltpu.roll(value, 4, 0)
        u_v[t, 0:4, :] = value[0:4]
        u_v[height - 1 - t, 4:8, :] = turned[4:8]

    @pl.loop(0, height // 8)
    def _(i):
        for k in range(8):
            conv_step(i * 8 + k)

    prepare(height, 1, dir_v, u_v, d_v, p_v, False)

    def col_body(t, state):
        return step(
            t, state, u_v, d_v, p_v, rate_v, ya_v, yb_v, height - 1, states, rank + states
        )

    state = lax.fori_loop(
        0, height // 2, col_body, tuple(jnp.zeros((8, chans), f32) for _ in range(states)), unroll=UNROLL
    )

    skip_v = skip_ref[2:3, :] + skip_ref[3:4, :]

    def column_row(t):
        at = pl.ds(pl.multiple_of(t * 8, 8), 8)
        parts = [
            ya_v[k, at, :] + pltpu.roll(yb_v[k, at, :], 4, 0) for k in range(chans // 128)
        ]
        return jnp.concatenate(parts, axis=1) + skip_v * u_v[t]

    def column_tile(j):
        tile = jnp.where(low4, column_row(2 * j), pltpu.roll(column_row(2 * j + 1), 4, 0))
        return jnp.concatenate([tile[:, 0:128], tile[:, 128:256]], axis=0).astype(bf16)

    def col_part(c, state):
        for k in range(8):
            state = col_body(height // 2 + 8 * c + k, state)
        for k in range(4):
            for j in (n // 2 - 4 - 4 * c + k, n // 2 + 4 * c + k):
                vsend[j] = column_tile(j)

                @pl.when(j != me)
                def _():
                    v_copy(j, me).start()

        return state

    lax.fori_loop(0, height // 16, col_part, state)

    vrecv[pl.ds(me, 1)] = vsend[pl.ds(me, 1)]

    row_steps(BEFORE, cols, tuple(state_h[s] for s in range(half)))

    @pl.loop(1, n)
    def _(d):
        other = lax.rem(me + d, n)
        v_copy(other, other).wait()

    skip_h = skip_ref[0:1, :] + skip_ref[1:2, :]

    def finish(p):
        even, other = vrecv[2 * p].astype(f32), vrecv[2 * p + 1].astype(f32)
        even = jnp.concatenate([even[0:8], even[8:16]], axis=1)
        other = jnp.concatenate([other[0:8], other[8:16]], axis=1)
        at = pl.ds(pl.multiple_of(p * 8, 8), 8)
        for r in range(rows):
            if r == 0:
                upright = jnp.where(low4, even, pltpu.roll(other, 4, 0))
            else:
                upright = jnp.where(low4, pltpu.roll(even, 4, 0), other)
            flat = skip_h * cr[r, at, :]
            for source, line in ((ya_h, r), (ya_h, 4 + r), (yb_h, 2 + r), (yb_h, 6 + r)):
                parts = [
                    source[k, pl.ds(p * 64 + line, 8, stride=8), :]
                    for k in range(chans // 128)
                ]
                flat = flat + jnp.concatenate(parts, axis=1)
            combined = flat + upright
            mean = jnp.sum(combined, axis=1, keepdims=True) / chans
            var = jnp.sum(combined * combined, axis=1, keepdims=True) / chans - mean * mean
            scaled = (combined - mean) * lax.rsqrt(var + 1e-05)
            normed[r, at, :] = scaled * gain_ref[...] + nbias_ref[...]

    @pl.loop(0, cols // 32)
    def _(i):
        for k in range(4):
            finish(4 * i + k)

    for r in range(rows):
        xs[pl.ds(r, chans, stride=rows), :] = normed[r].T
    out_ref[...] = (xs[...] * jax.nn.silu(gate_ref[...].astype(f32))).astype(bf16)


def fused_device(
    n,
    x_in,
    gate_in,
    conv_weight,
    conv_bias,
    proj_weight,
    dt_weight,
    dt_bias,
    decay_rate,
    skip_gain,
    norm_gain,
    norm_bias,
):
    chans, rows, cols = x_in.shape
    states = decay_rate.shape[2]
    height = rows * n
    f32, bf16 = jnp.float32, jnp.bfloat16
    scratch = [
        pltpu.VMEM((chans * rows, cols), f32),
        pltpu.VMEM((rows, cols, chans), bf16),
        pltpu.VMEM((rows, cols, chans), f32),
        pltpu.VMEM((rows + 2, cols + 16, chans), f32),
        pltpu.VMEM((2, cols, chans), bf16),
        pltpu.VMEM((n, 24, 128), bf16),
        pltpu.VMEM((n, 24, 128), bf16),
        pltpu.VMEM((height + 2, 8, chans), f32),
        pltpu.VMEM((rows, cols, chans), f32),
        pltpu.VMEM((512, chans), f32),
        pltpu.VMEM((2, chans, 256), bf16),
        pltpu.VMEM((512, chans), f32),
        pltpu.VMEM((states // 2, 8, chans), f32),
        pltpu.VMEM((states, 8, chans), f32),
        pltpu.VMEM((cols, 8, chans), f32),
        pltpu.VMEM((cols, 8, chans), f32),
        pltpu.VMEM((cols, 8, 128), f32),
        pltpu.VMEM((chans // 128, cols * 8, 128), f32),
        pltpu.VMEM((chans // 128, cols * 8, 128), f32),
        pltpu.VMEM((states // 2, 8, chans), f32),
        pltpu.VMEM((height, 8, chans), f32),
        pltpu.VMEM((height, 8, chans), f32),
        pltpu.VMEM((height, 8, 128), f32),
        pltpu.VMEM((chans // 128, height * 8, 128), f32),
        pltpu.VMEM((chans // 128, height * 8, 128), f32),
        pltpu.VMEM((n, 16, 128), bf16),
        pltpu.VMEM((n, 16, 128), bf16),
        pltpu.SemaphoreType.DMA((2,)),
        pltpu.SemaphoreType.DMA((2,)),
        pltpu.SemaphoreType.DMA((n,)),
        pltpu.SemaphoreType.DMA((n,)),
        pltpu.SemaphoreType.DMA((n,)),
        pltpu.SemaphoreType.DMA((n,)),
    ]
    operands = (
        x_in.reshape(chans * rows, cols),
        conv_weight.T,
        conv_bias[None, :],
        proj_weight,
        dt_weight.transpose(0, 2, 1),
        dt_bias,
        decay_rate.transpose(0, 2, 1),
        skip_gain,
        norm_gain[None, :],
        norm_bias[None, :],
        gate_in.reshape(chans * rows, cols),
    )
    held = [pltpu.VMEM(a.shape, a.dtype) for a in operands]
    mixed = pl.pallas_call(
        functools.partial(fused_kernel, n),
        out_shape=jax.ShapeDtypeStruct((chans * rows, cols), bf16),
        in_specs=[pl.BlockSpec(memory_space=pltpu.HBM)] * len(operands),
        out_specs=pl.BlockSpec(memory_space=pltpu.VMEM),
        scratch_shapes=held + scratch + [pltpu.SemaphoreType.DMA((len(operands),))],
        compiler_params=pltpu.CompilerParams(
            collective_id=0, has_side_effects=True, vmem_limit_bytes=64 * 1024 * 1024
        ),
    )(*operands)
    return mixed.reshape(chans, rows, cols)


def on_device(*args):
    n = lax.axis_size("sp")
    chans, rows, cols = args[0].shape
    rank, states = args[5].shape[2], args[7].shape[2]
    fits = (chans, rows, cols, rank, states) == (256, 2, 4 * n, 8, 16)
    if lax.axis_size("ch") == 1 and fits:
        return fused_device(n, *args)
    return plain_device(*args)


def solution(mesh):
    placed = (
        P("ch", "sp", None),
        P("ch", "sp", None),
        P("ch", None),
        P("ch"),
        P(None, None, "ch"),
        P(None, "ch", None),
        P(None, "ch"),
        P(None, "ch", None),
        P(None, "ch"),
        P("ch"),
        P("ch"),
    )
    return jax.shard_map(
        on_device, mesh=mesh, in_specs=placed, out_specs=P("ch", "sp", None), check_vma=False
    )
```
